256 devices in a mesh: grp: 8 (over z_hi, y), dev: 32 (over x, z_lo, core).
Axes of the slice: x: 4, y: 4, z: 8 (z_hi: 2, z_lo: 4; z = z_hi * 4 + z_lo), core: 2. Of those that a mesh axis runs over, the one named last changes fastest.
Arguments:
- hidden_in: bfloat16 [256, 256, 1024], P(('grp', 'dev'))
- w_query: bfloat16 [1024, 1024], P('grp'), may hold values from -0.1875 to 0.1875
- w_keyval: bfloat16 [1024, 2048], P('grp'), may hold values from -0.1875 to 0.1875
- w_out: bfloat16 [1024, 1024], P('grp'), may hold values from -0.1875 to 0.1875
- ln_gain: float32 [1024], replicated, may hold values from 0.1 to 1.9
- ln_bias: float32 [1024], replicated, may hold values from -3 to 3
- bank: bfloat16 [65536, 1024], P(('grp', 'dev')), may hold values from -6 to 6
- owner: int32 [256], P(('grp', 'dev')), may hold values from 0 to 255, as said below
- slot: int32 [256], P(('grp', 'dev')), may hold values from 0 to 255
Outputs:
- updated: bfloat16 [65536, 1024], P(('grp', 'dev'))
The draws below stay inside these ranges and needn't reach their ends.
Inputs may be any that keep to these rules, and one draw needn't show every extreme that they name: `owner`: each device owns at most 8 sampled passages, and some device owns exactly 8.
All inputs are finite; a program needn't handle non-finite values.
Results may differ from the reference program's by a relative error of at most 0.012.
The reference program's roundings to bfloat16 on the way (of `keyval`, `query`, `probs`, `context`, `fresh`, `old` and `adapter`) count: a program that leaves them out, or rounds other values in their place, can miss the bound.
Values may be sent and summed in bfloat16 or wider, within the bound.
No kernel may reach another device: no remote copies, remote signals or barrier semaphores. Data moves between devices by JAX's collectives and lax.ppermute only.
A program may use at most 128 MiB of HBM per device.

```python
import jax
import jax.numpy as jnp
from jax import lax

D = 1024
HEADS = 16
HEAD = 64
L = 256
SLAB = 256
MOST = 8
BANK_DEVICES = 256
SAMPLES = 256
BANK_ROWS = 65536


def draw_hidden_in(key, part):
    key = jax.random.fold_in(key, 5)
    first = jax.random.fold_in(key, 0)
    values = jnp.clip(jax.random.normal(first, (SAMPLES, L, D), jnp.float32), -6.0, 6.0)
    return values.astype(jnp.bfloat16)


def draw_owner(key, part):
    key = jax.random.fold_in(key, 11)
    first, second, third = jax.random.split(key, 3)
    pool_size = BANK_DEVICES * MOST
    chosen_device = jax.random.randint(first, (), 0, BANK_DEVICES)
    positions = jnp.arange(pool_size, dtype=jnp.int32)
    device_of = positions // MOST
    scores = jax.random.permutation(second, pool_size).astype(jnp.int32)
    scores = jnp.where(device_of == chosen_device, -1 - positions % MOST, scores)
    order = jnp.argsort(scores, stable=True)
    picked = device_of[order[:SAMPLES]]
    return jax.random.permutation(third, picked).astype(jnp.int32)


def touch_ends(drawn, rng, smallest, top_value):
    extent = drawn.shape
    spot = [jax.random.randint(jax.random.fold_in(rng, axis), (), 0, extent[axis]) for axis in range(len(extent))]
    drawn = drawn.at[tuple(spot)].set(smallest)
    longest = extent.index(max(extent))
    spot[longest] = (spot[longest] + 1) % extent[longest]
    return drawn.at[tuple(spot)].set(top_value)


def level_of(rng, extent, cuts, low, largest):
    def one(position, blocks):
        draws = jax.random.uniform(jax.random.fold_in(jax.random.fold_in(rng, 6), position), (blocks,), jnp.float32, low / len(cuts), largest / len(cuts))
        return jnp.repeat(jnp.exp(draws), extent[position] // blocks).reshape((-1,) + (1,) * (len(extent) - position - 1))

    gain = one(*cuts[0])
    for cut in cuts[1:]:
        gain = gain * one(*cut)
    return gain


def normal_values(key, dims, spread, limit, shards=(), kind=jnp.bfloat16):
    result = spread * jax.random.normal(key, dims, jnp.float32)
    if shards:
        result = result * level_of(key, dims, shards, -0.22, 0.18)
    return jnp.clip(result, -limit, limit).astype(kind)


def setup_inputs(seed: int = 0) -> dict:
    arg_keys = jax.random.split(jax.random.key(seed), 10)
    hidden_in = draw_hidden_in(jax.random.fold_in(arg_keys[9], 71), 0)
    w_query = normal_values(arg_keys[1], (D, D), D ** -0.5, 0.1875, ((0, 8),))
    w_keyval = normal_values(arg_keys[2], (D, 2 * D), D ** -0.5, 0.1875, ((0, 8),))
    w_out = normal_values(arg_keys[3], (D, D), D ** -0.5, 0.1875, ((0, 8),))
    ln_gain = jnp.clip(1.0 + 0.18 * jax.random.normal(arg_keys[4], (D,), jnp.float32), 0.1, 1.9)
    ln_bias = normal_values(arg_keys[5], (D,), 0.5, 3.0, (), jnp.float32)
    bank = normal_values(arg_keys[6], (BANK_ROWS, D), 1.0, 6.0, ((0, 256),))
    owner = draw_owner(jax.random.fold_in(arg_keys[9], 71), 0)
    slot = touch_ends(jax.random.randint(arg_keys[8], (SAMPLES,), 0, SLAB), jax.random.fold_in(arg_keys[8], 1), 0, SLAB - 1).astype(jnp.int32)
    return {"hidden_in": hidden_in, "w_query": w_query, "w_keyval": w_keyval, "w_out": w_out, "ln_gain": ln_gain, "ln_bias": ln_bias, "bank": bank, "owner": owner, "slot": slot}


def encode_block(block, w_query, w_keyval, w_out, ln_gain, ln_bias):
    count = block.shape[0]
    flat = block.reshape(count * L, D)
    keyval = jnp.dot(flat.astype(jnp.float32), w_keyval.astype(jnp.float32), preferred_element_type=jnp.float32).astype(jnp.bfloat16)
    keyval = keyval.reshape(count, L, 2, HEADS, HEAD)
    cls = block[:, 0, :]
    query = (0.125 * jnp.dot(cls.astype(jnp.float32), w_query.astype(jnp.float32), preferred_element_type=jnp.float32)).astype(jnp.bfloat16)
    query = query.reshape(count, HEADS, HEAD)
    scores = jnp.einsum('she,slhe->shl', query.astype(jnp.float32), keyval[:, :, 0].astype(jnp.float32))
    probs = jax.nn.softmax(scores, axis=-1).astype(jnp.bfloat16)
    context = jnp.einsum('shl,slhe->she', probs.astype(jnp.float32), keyval[:, :, 1].astype(jnp.float32))
    context = context.astype(jnp.bfloat16).reshape(count, D)
    joined = cls.astype(jnp.float32) + jnp.dot(context.astype(jnp.float32), w_out.astype(jnp.float32), preferred_element_type=jnp.float32)
    center = joined - lax.optimization_barrier(jnp.mean(joined, axis=-1, keepdims=True))
    normed = center / jnp.sqrt(lax.optimization_barrier(jnp.mean(center * center, axis=-1, keepdims=True)) + 1e-05) * ln_gain + ln_bias
    fresh = normed / jnp.sqrt(lax.optimization_barrier(jnp.mean(normed * normed, axis=-1, keepdims=True)) + 1e-06)
    return fresh.astype(jnp.bfloat16)

def reference(hidden_in, w_query, w_keyval, w_out, ln_gain, ln_bias, bank, owner, slot):
    blocks = hidden_in.reshape(SAMPLES // 8, 8, L, D)
    fresh = lax.map(lambda b: encode_block(b, w_query, w_keyval, w_out, ln_gain, ln_bias), blocks)
    fresh = fresh.reshape(SAMPLES, D)
    rows = owner.astype(jnp.int32) * SLAB + slot.astype(jnp.int32)
    old = bank[rows]
    gram = jnp.einsum('md,me->de', old.astype(jnp.float32), old.astype(jnp.float32), preferred_element_type=jnp.float32)
    cross = jnp.einsum('md,me->de', old.astype(jnp.float32), fresh.astype(jnp.float32), preferred_element_type=jnp.float32)
    system = gram + 0.25 * SAMPLES * jnp.eye(D, dtype=jnp.float32)
    factor = jnp.linalg.cholesky(system)
    adapter = jax.scipy.linalg.cho_solve((factor, True), cross).astype(jnp.bfloat16)
    return jnp.dot(bank.astype(jnp.float32), adapter.astype(jnp.float32), preferred_element_type=jnp.float32).astype(jnp.bfloat16)
```

```python
import jax
import jax.numpy as jnp
from jax import lax
from jax.experimental import pallas as pl
from jax.experimental.pallas import tpu as pltpu
from jax.sharding import PartitionSpec as P

HEADS = 16
HEAD = 64
WIDTH = 1024
CUT = 128
PLANE = 32
BF = jnp.bfloat16
F32 = jnp.float32
NT = (((1,), (1,)), ((), ()))
TN = (((0,), (0,)), ((), ()))


def plane(apart=False):
    split = [(0,), (1,)] if apart else [(0, 1)]
    return [
        [(zh * 4 + y) * 32 + x * 8 + zl * 2 + c for y in range(4) for x in range(4) for c in cores]
        for zh in range(2)
        for zl in range(4)
        for cores in split
    ]


def exchange(x, groups):
    return lax.all_to_all(x, ("grp", "dev"), split_axis=0, concat_axis=0, tiled=True, axis_index_groups=groups)


def spread(x, groups):
    return exchange(jnp.broadcast_to(x[None], (len(groups[0]), *x.shape)), groups)


def after(x, *others):
    return lax.optimization_barrier((x, *others))[0]


def call(kernel, out, flops, *args, where=None, scratch=(), hbm=False, mib=12):
    vmem = pl.BlockSpec(memory_space=pltpu.VMEM)
    first = [] if where is None else [where]
    return pl.pallas_call(
        kernel,
        out_shape=out,
        in_specs=[pl.BlockSpec(memory_space=pltpu.SMEM)] * len(first)
        + [pl.BlockSpec(memory_space=pltpu.HBM) if hbm else vmem] * len(args),
        out_specs=jax.tree.map(lambda _: vmem, out),
        scratch_shapes=list(scratch),
        compiler_params=pltpu.CompilerParams(vmem_limit_bytes=mib * 2**20),
        cost_estimate=pl.CostEstimate(flops=flops, bytes_accessed=2**20, transcendentals=0),
    )(*first, *args)


def shape(dims, kind):
    return jax.ShapeDtypeStruct(dims, kind)


def dot(a, b, dims=(((1,), (0,)), ((), ()))):
    return lax.dot_general(a, b, dims, preferred_element_type=F32)


def exact(a, b):
    return jnp.dot(a, b, preferred_element_type=F32, precision=lax.Precision.HIGHEST)


def terms(x):
    high = x.astype(BF)
    rest = x - high.astype(F32)
    mid = rest.astype(BF)
    return high, mid, (rest - mid.astype(F32)).astype(BF)


def stack(refs):
    return jnp.concatenate([r[...].astype(F32) for r in refs], axis=0)


def head_mask(rows):
    row = lax.broadcasted_iota(jnp.int32, (rows, 4 * HEAD), 0)
    col = lax.broadcasted_iota(jnp.int32, (rows, 4 * HEAD), 1)
    return lax.rem(row, 4) == lax.div(col, HEAD)


def cut_kernel(where, query_ref, keyval_ref, own_ref, sent_ref, sems):
    zl, c = where[2], where[3]
    copies = []
    for ref, block in ((sent_ref, 4 * c + 3 - zl), (own_ref, 4 * c + zl)):
        at = pl.multiple_of(block * CUT, CUT)
        value_at = pl.multiple_of(block * CUT + WIDTH, CUT)
        parts = (query_ref.at[:, pl.ds(at, CUT)], keyval_ref.at[:, pl.ds(at, CUT)])
        for i, source in enumerate((*parts, keyval_ref.at[:, pl.ds(value_at, CUT)])):
            target = ref.at[:, i * CUT : (i + 1) * CUT]
            copies.append(pltpu.make_async_copy(source, target, sems.at[len(copies)]))
            copies[-1].start()
    for copy in copies:
        copy.wait()


def pick_kernel(where, near_ref, far_ref, bank_ref, keep_ref, give_ref, select_ref):
    info = jnp.concatenate([near_ref[...], far_ref[...]], axis=0)
    n = bank_ref.shape[0]
    number = lax.broadcasted_iota(jnp.int32, (n, n), 1).astype(F32)
    own, slot, place = [info[:, i : i + 1] for i in range(3)]
    a = jnp.where((place == number) & (own == where[7].astype(F32)), 1.0, 0.0).astype(BF)
    b = jnp.where(slot == number, 1.0, 0.0).astype(BF)
    select_ref[...] = dot(a, b, TN)
    for ref, c in ((keep_ref, where[3]), (give_ref, 1 - where[3])):
        select = select_ref[pl.ds(pl.multiple_of(c * (n // 2), n // 2), n // 2), :].astype(BF)
        ref[...] = dot(select, bank_ref[...]).astype(BF)


def row_blocks(where):
    zh, y = where[0], where[1]
    for k in range(4):
        yk = lax.rem(y + 4 - k, 4)
        for h in range(2):
            at = ((zh if h == 0 else 1 - zh) * 4 + yk) * CUT
            yield k, slice(h * CUT, (h + 1) * CUT), pl.ds(pl.multiple_of(at, CUT), CUT)


def cls_row(ref):
    return jnp.concatenate([ref[i : i + 1, :] for i in range(8)], axis=1)


def key_kernel(where, c0, c1, c2, c3, n0, n1, n2, n3, f0, f1, f2, f3, u0, u1, u2, u3, cls_ref):
    near, far = (n0, n1, n2, n3), (f0, f1, f2, f3)
    for k, ref in enumerate((c0, c1, c2, c3)):
        cls_ref[k : k + 1, :] = cls_row(ref)
    query = jnp.zeros((4, 4 * HEAD), F32)
    for k, rows, features in row_blocks(where):
        cls = cls_ref[0:4, features].astype(BF)
        query += jnp.concatenate([dot(cls, near[k][rows, :CUT]), dot(cls, far[k][rows, :CUT])], axis=1)
    query = (0.125 * query).astype(BF).astype(F32)
    query = jnp.concatenate([jnp.broadcast_to(query[k : k + 1], (4, 4 * HEAD)) for k in range(4)], axis=0)
    query = jnp.where(head_mask(16), query, 0.0).astype(BF)
    for k, rows, features in row_blocks(where):
        u = dot(query[:, :CUT], near[k][rows, CUT : 2 * CUT], NT) + dot(
            query[:, CUT:], far[k][rows, CUT : 2 * CUT], NT
        )
        for j, ref in enumerate((u0, u1, u2, u3)):
            ref[:, features] = u[4 * j : 4 * j + 4]


def attend_kernel(x_ref, u0, u1, u2, u3, y0, y1, y2, y3):
    x = x_ref[...]
    parts = dot(jnp.concatenate(terms(stack((u0, u1, u2, u3))), axis=0), x, NT)
    scores = parts[2 * HEADS :] + parts[HEADS : 2 * HEADS] + parts[:HEADS]
    e = jnp.exp(scores - jnp.max(scores, axis=1, keepdims=True))
    probs = (e / jnp.sum(e, axis=1, keepdims=True)).astype(BF)
    y = dot(probs, x)
    for k, ref in enumerate((y0, y1, y2, y3)):
        ref[...] = y[4 * k : 4 * k + 4]


def value_kernel(
    where, y0, y1, y2, y3, n0, n1, n2, n3, f0, f1, f2, f3, out_ref, out2_ref, old_ref, part_ref, y_ref
):
    near, far = (n0, n1, n2, n3), (f0, f1, f2, f3)
    y_ref[...] = jnp.concatenate(terms(stack((y0, y1, y2, y3))), axis=0)
    parts = jnp.zeros((3 * HEADS, 4 * HEAD), F32)
    for k, rows, features in row_blocks(where):
        y = y_ref[:, features]
        parts += jnp.concatenate([dot(y, near[k][rows, 2 * CUT :]), dot(y, far[k][rows, 2 * CUT :])], axis=1)
    parts = jnp.where(head_mask(HEADS), parts[2 * HEADS :] + parts[HEADS : 2 * HEADS] + parts[:HEADS], 0.0)
    context = [jnp.sum(parts[4 * k : 4 * k + 4], axis=0, keepdims=True) for k in range(4)]
    context = jnp.concatenate(context, axis=0).astype(BF)
    part = dot(context[:, :CUT], out_ref[...]) + dot(context[:, CUT:], out2_ref[...])
    part_ref[0:8, :] = jnp.zeros((8, WIDTH), F32)
    for k in range(4):
        part_ref[pl.ds(lax.rem(where[2] + 4 - k, 4), 1), :] = part[k : k + 1]
    part_ref[8:16, :] = jnp.sum(old_ref[...].astype(F32), axis=0)


def norm_kernel(where, t0, t1, t2, t3, c0, c1, c2, c3, gain_ref, bias_ref, rows_ref, cls_ref):
    for k, ref in enumerate((c0, c1, c2, c3)):
        cls_ref[pl.ds(lax.rem(where[2] + 4 - k, 4), 1), :] = cls_row(ref)
    total = (t0[...] + t1[...]) + (t2[...] + t3[...])
    joined = cls_ref[0:4, :] + total[0:4]
    center = joined - jnp.mean(joined, axis=-1, keepdims=True)
    var = jnp.mean(center * center, axis=-1, keepdims=True)
    normed = center / jnp.sqrt(var + 1e-05) * gain_ref[...] + bias_ref[...]
    fresh = normed / jnp.sqrt(jnp.mean(normed * normed, axis=-1, keepdims=True) + 1e-06)
    rows_ref[...] = jnp.concatenate([fresh, jnp.zeros_like(fresh), total[8:]], axis=0).astype(BF)


def product(a, b):
    a1, a2, _ = terms(a)
    b1, b2, _ = terms(b)
    return dot(a2, b1) + dot(a1, b2) + dot(a1, b1)


def update_kernel(old_ref, fresh_ref, bank_ref, out_ref):
    old = old_ref[...]
    n = old.shape[0]
    rows = lax.broadcasted_iota(jnp.int32, (n, n), 0)
    cols = lax.broadcasted_iota(jnp.int32, (n, n), 1)
    eye = jnp.where(rows == cols, 1.0, 0.0).astype(F32)
    ridge = 0.25 * n
    a = dot(old, old, NT) + ridge * eye
    norm = jnp.max(jnp.sum(jnp.abs(a), axis=1, keepdims=True))
    c = 2.0 / (ridge + norm)
    r = eye - c * a
    x = c * (eye + r)

    def size(r):
        return jnp.max(jnp.sum(jnp.abs(r), axis=1, keepdims=True))

    def step(times, state):
        t, _, x, r = state
        both = times(jnp.concatenate([x, r], axis=0), r)
        r = both[n:]
        return 2.0 * t, size(r), x + both[:n], r

    def more(state):
        return (state[0] < 9.0) & (state[1] > 1e-4)

    r = exact(r, r)
    state = (2.0 * c * ridge, size(r), x, r)
    state = lax.while_loop(lambda s: more(s) & (norm < 512.0 * ridge), lambda s: step(product, s), state)
    x = lax.while_loop(more, lambda s: step(exact, s), state)[2]

    def refine(state):
        i, _, x = state
        e = eye - exact(a, x)
        return i + 1, jnp.sum(e * e), x + exact(x, e)

    _, _, x = lax.while_loop(
        lambda s: (s[0] == 0) | ((s[1] > 1e-7) & (s[0] < 4)), refine, (jnp.int32(0), jnp.float32(1.0), x)
    )
    high, mid, low = terms(x)
    fresh = fresh_ref[...]
    z1, z2, z3 = terms(dot(low, fresh) + dot(mid, fresh) + dot(high, fresh))
    adapter = (dot(old, z3, TN) + dot(old, z2, TN) + dot(old, z1, TN)).astype(BF)
    out_ref[...] = dot(bank_ref[...], adapter).astype(BF)


def shift(x, move):
    perm = []
    for i in range(256):
        zh, y, xx, zl, c = i // 128, i // 32 % 4, i // 8 % 4, i // 2 % 4, i % 2
        zh, y, xx, zl, c = move(zh, y, xx, zl, c)
        perm.append((i, (((zh % 2) * 4 + y % 4) * 4 + xx % 4) * 8 + (zl % 4) * 2 + c % 2))
    return lax.ppermute(x, ("grp", "dev"), perm)


def along_y(x, k):
    return shift(x, lambda zh, y, xx, zl, c: (zh, y + k, xx, zl, c)) if k % 4 else x


def along_z(x, k):
    return shift(x, lambda zh, y, xx, zl, c: (zh, y, xx, zl + k, c)) if k % 4 else x


def other_core(x):
    return shift(x, lambda zh, y, xx, zl, c: (zh, y, xx, zl, c + 1))


def mirror(x):
    return shift(x, lambda zh, y, xx, zl, c: (zh + 1, y, xx, 3 - zl, c))


def local(hidden_in, w_query, w_keyval, w_out, ln_gain, ln_bias, bank, owner, slot):
    hidden = hidden_in[0]
    grp, dev = lax.axis_index("grp"), lax.axis_index("dev")
    zh, y, zl, c = grp // 4, grp % 4, dev // 2 % 4, dev % 2
    place = ((c * 4 + y) * 4 + dev // 8) * 8 + zh * 4 + zl
    where = jnp.stack([zh, y, zl, c, owner[0], slot[0], place, grp * 32 + dev])

    lane = lax.broadcasted_iota(jnp.int32, (1, 128), 1)
    info = jnp.where(lane == 0, where[4], jnp.where(lane == 1, where[5], where[6])).astype(F32)
    info = spread(info, plane()).reshape(PLANE, 128)

    own, sent = call(
        cut_kernel,
        [shape((CUT, 3 * CUT), BF)] * 2,
        2**10,
        w_query,
        w_keyval,
        where=where,
        scratch=[pltpu.SemaphoreType.DMA((6,))],
        hbm=True,
    )
    out1 = shift(w_out, lambda zh, y, xx, zl, c: (c, zl, xx, y, zh))
    own = jnp.concatenate([own, mirror(after(sent, info, out1))], axis=0)
    out2 = other_core(out1)
    near = [along_y(own, k) for k in range(4)]
    far = [other_core(w) for w in near]
    cls = jnp.concatenate([hidden[:1].astype(F32).reshape(8, 128), info], axis=0)
    cls = [along_z(cls, k) for k in range(4)]
    info = jnp.concatenate([p[8:] for p in cls], axis=0)
    half = shape((bank.shape[0] // 2, WIDTH), BF)
    keep, give = call(
        pick_kernel,
        [half, half],
        2**28,
        info,
        mirror(info),
        bank,
        where=where,
        scratch=[pltpu.VMEM((bank.shape[0], bank.shape[0]), F32)],
    )
    rows = keep + other_core(give)

    u = call(
        key_kernel,
        [shape((4, WIDTH), F32)] * 4,
        2**23,
        *cls,
        *near,
        *far,
        where=where,
        scratch=[pltpu.VMEM((8, WIDTH), F32)],
    )
    u = [along_z(a, -k) for k, a in enumerate(u)]
    rows = exchange(after(rows, *u[1:]).reshape(PLANE // 2, 8, WIDTH), plane(apart=True))
    y = call(attend_kernel, [shape((4, WIDTH), F32)] * 4, 2**25, hidden, *u)
    y = [along_z(a, k) for k, a in enumerate(y)]
    part = call(
        value_kernel,
        shape((16, WIDTH), F32),
        2**24,
        *y,
        *near,
        *far,
        out1,
        out2,
        rows,
        where=where,
        scratch=[pltpu.VMEM((3 * HEADS, WIDTH), BF)],
    )
    part = [along_z(part, k) for k in range(4)]
    mine = call(
        norm_kernel,
        shape((16, WIDTH), BF),
        2**14,
        *part,
        *cls,
        ln_gain.reshape(1, -1),
        ln_bias.reshape(1, -1),
        where=where,
        scratch=[pltpu.VMEM((8, WIDTH), F32)],
    )
    other = mirror(mine)
    low = jnp.where(zh == 0, mine[:4], other[:4])
    high = jnp.where(zh == 0, other[:4], mine[:4])
    both = spread(jnp.concatenate([low, high, mine[8:] + other[8:]], axis=0), plane(apart=True))
    both = jnp.concatenate([both, other_core(both)], axis=0)
    fresh, old = both[:, :8].reshape(256, WIDTH), both[:, 8:].reshape(256, WIDTH)
    return call(update_kernel, shape(bank.shape, BF), 2**31, old, fresh, bank, mib=32)


def solution(mesh):
    in_specs = (
        P(("grp", "dev"), None, None),
        P("grp", None),
        P("grp", None),
        P("grp", None),
        P(),
        P(),
        P(("grp", "dev"), None),
        P(("grp", "dev")),
        P(("grp", "dev")),
    )
    out_specs = P(("grp", "dev"), None)
    return jax.shard_map(local, mesh=mesh, in_specs=in_specs, out_specs=out_specs, check_vma=False)
```

```python
import jax
import jax.numpy as jnp
from jax import lax
from jax.experimental import pallas as pl
from jax.experimental.pallas import tpu as pltpu
from jax.sharding import PartitionSpec as P

HEAD = 64
WIDTH = 1024
CUT = 128
PLACES = 256
BF = jnp.bfloat16
F32 = jnp.float32
NT = (((1,), (1,)), ((), ()))
TN = (((0,), (0,)), ((), ()))


def columns(cores):
    return [
        [(zh * 4 + y) * 32 + x * 8 + zl * 2 + c for zh in range(2) for zl in range(4) for y in range(4) for c in cs]
        for x in range(4)
        for cs in ([(0, 1)] if cores == 2 else [(0,), (1,)])
    ]


def exchange(x, cores):
    return lax.all_to_all(
        x, ("grp", "dev"), split_axis=0, concat_axis=0, tiled=True, axis_index_groups=columns(cores)
    )


def spread(x, cores):
    return exchange(jnp.broadcast_to(x[None], (32 * cores, *x.shape)), cores)


def after(x, *others):
    return lax.optimization_barrier((x, *others))[0]


def call(kernel, out, flops, *args, where=None, scratch=(), hbm=(), mib=12):
    vmem = pl.BlockSpec(memory_space=pltpu.VMEM)
    first = [] if where is None else [where]
    return pl.pallas_call(
        kernel,
        out_shape=out,
        in_specs=[pl.BlockSpec(memory_space=pltpu.SMEM)] * len(first)
        + [pl.BlockSpec(memory_space=pltpu.HBM) if i in hbm else vmem for i in range(len(args))],
        out_specs=jax.tree.map(lambda _: vmem, out),
        scratch_shapes=list(scratch),
        compiler_params=pltpu.CompilerParams(vmem_limit_bytes=mib * 2**20),
        cost_estimate=pl.CostEstimate(flops=flops, bytes_accessed=2**20, transcendentals=0),
    )(*first, *args)


def shape(dims, kind):
    return jax.ShapeDtypeStruct(dims, kind)


def dot(a, b, dims=(((1,), (0,)), ((), ()))):
    return lax.dot_general(a, b, dims, preferred_element_type=F32)


def exact(a, b):
    return jnp.dot(a, b, preferred_element_type=F32, precision=lax.Precision.HIGHEST)


def terms(x):
    high = x.astype(BF)
    rest = x - high.astype(F32)
    mid = rest.astype(BF)
    return high, mid, (rest - mid.astype(F32)).astype(BF)


def head_mask(rows):
    row = lax.broadcasted_iota(jnp.int32, (rows, 4 * HEAD), 0)
    col = lax.broadcasted_iota(jnp.int32, (rows, 4 * HEAD), 1)
    return lax.rem(row, 4) == lax.div(col, HEAD)


def cut_kernel(where, query_ref, keyval_ref, own_ref):
    block = 4 * where[3] + where[2]
    at = pl.ds(pl.multiple_of(block * CUT, CUT), CUT)
    own_ref[:, :CUT] = query_ref[:, at]
    own_ref[:, CUT : 2 * CUT] = keyval_ref[:, at]
    own_ref[:, 2 * CUT :] = keyval_ref[:, pl.ds(pl.multiple_of(block * CUT + WIDTH, CUT), CUT)]


def pick_kernel(where, info_ref, bank_ref, rows_ref):
    n = bank_ref.shape[0]
    number = lax.broadcasted_iota(jnp.int32, (PLACES, n), 1).astype(F32)
    own, slot, place = [info_ref[:, i : i + 1] for i in range(3)]
    a = jnp.where((place == number) & (own == where[6].astype(F32)), 1.0, 0.0).astype(BF)
    b = jnp.where(slot == number, 1.0, 0.0).astype(BF)
    rows_ref[...] = dot(dot(a, b, TN).astype(BF), bank_ref[...]).astype(BF)


def row_blocks(where):
    zh, y = where[0], where[1]
    for k in range(4):
        yk = lax.rem(y + 4 - k, 4)
        for h in range(2):
            at = ((zh if h == 0 else 1 - zh) * 4 + yk) * CUT
            yield k, slice(h * CUT, (h + 1) * CUT), pl.ds(pl.multiple_of(at, CUT), CUT)


def encode_kernel(
    where, h0, h1, h2, h2b, h3, n0, n1, n2, n3, f0, f1, f2, f3, out_ref, out2_ref, part_ref, w_ref
):
    near, far = (n0, n1, n2, n3), (f0, f1, f2, f3)
    for k, rows, features in row_blocks(where):
        for i in range(3):
            cols = slice(i * CUT, (i + 1) * CUT)
            w_ref[features, 2 * i * CUT : (2 * i + 1) * CUT] = near[k][rows, cols]
            w_ref[features, (2 * i + 1) * CUT : (2 * i + 2) * CUT] = far[k][rows, cols]
    four = 4 * HEAD
    mask = head_mask(4)
    contexts = []
    for refs in ((h0,), (h1,), (h2, h2b), (h3,)):
        x = jnp.concatenate([r[...] for r in refs], axis=0)
        keyval = dot(x, w_ref[:, four:]).astype(BF)
        query = (0.125 * dot(x[0:16], w_ref[:, :four])[0:1]).astype(BF).astype(F32)
        query = jnp.where(mask, jnp.broadcast_to(query, (4, four)), 0.0).astype(BF)
        scores = dot(query, keyval[:, :four], NT)
        e = jnp.exp(scores - jnp.max(scores, axis=1, keepdims=True))
        probs = (e / jnp.sum(e, axis=1, keepdims=True)).astype(BF)
        context = jnp.where(mask, dot(probs, keyval[:, four:]), 0.0)
        contexts.append(jnp.sum(context, axis=0, keepdims=True))
    context = jnp.concatenate(contexts, axis=0).astype(BF)
    part = dot(context[:, :CUT], out_ref[...]) + dot(context[:, CUT:], out2_ref[...])
    for k in range(4):
        row = part[k : k + 1]
        if k == 0:
            row = row + h0[0:1, :].astype(F32)
        part_ref[pl.ds(lax.rem(where[2] + 4 - k, 4), 1), :] = row


def pack_kernel(part_ref, old_ref, both_ref):
    both_ref[...] = jnp.concatenate([part_ref[...], jnp.sum(old_ref[...].astype(F32), axis=0)], axis=0)


def norm_kernel(t0, t1, t2, t3, gain_ref, bias_ref, rows_ref):
    total = (t0[...] + t1[...]) + (t2[...] + t3[...])
    joined = total[0:4]
    center = joined - jnp.mean(joined, axis=-1, keepdims=True)
    var = jnp.mean(center * center, axis=-1, keepdims=True)
    normed = center / jnp.sqrt(var + 1e-05) * gain_ref[...] + bias_ref[...]
    fresh = normed / jnp.sqrt(jnp.mean(normed * normed, axis=-1, keepdims=True) + 1e-06)
    rows_ref[...] = jnp.concatenate([fresh, total[4:8]], axis=0).astype(BF)


def product(a, b):
    a1, a2, _ = terms(a)
    b1, b2, _ = terms(b)
    return dot(a2, b1) + dot(a1, b2) + dot(a1, b1)


def update_kernel(here_ref, there_ref, bank_ref, out_ref):
    half = here_ref.shape[0] // 2
    row = lax.broadcasted_iota(jnp.int32, (half, 2 * half), 0)
    col = lax.broadcasted_iota(jnp.int32, (half, 2 * half), 1)
    at = lax.div(row, 4) * 8 + lax.rem(row, 4)

    def take(first):
        pick = jnp.where(col == at + first, 1.0, 0.0).astype(BF)
        return jnp.concatenate([dot(pick, ref[...]).astype(BF) for ref in (here_ref, there_ref)], axis=0)

    old, fresh = take(4), take(0)
    n = 2 * half
    rows = lax.broadcasted_iota(jnp.int32, (n, n), 0)
    cols = lax.broadcasted_iota(jnp.int32, (n, n), 1)
    eye = jnp.where(rows == cols, 1.0, 0.0).astype(F32)
    ridge = 0.25 * n
    a = dot(old, old, NT) + ridge * eye
    norm = jnp.max(jnp.sum(jnp.abs(a), axis=1, keepdims=True))
    c = 2.0 / (ridge + norm)
    r = eye - c * a
    x = c * (eye + r)

    def size(r):
        return jnp.max(jnp.sum(jnp.abs(r), axis=1, keepdims=True))

    def step(times, state):
        t, _, x, r = state
        both = times(jnp.concatenate([x, r], axis=0), r)
        r = both[n:]
        return 2.0 * t, size(r), x + both[:n], r

    def more(state):
        return (state[0] < 9.0) & (state[1] > 1e-4)

    r = exact(r, r)
    state = (2.0 * c * ridge, size(r), x, r)
    state = lax.while_loop(lambda s: more(s) & (norm < 512.0 * ridge), lambda s: step(product, s), state)
    x = lax.while_loop(more, lambda s: step(exact, s), state)[2]

    def refine(state):
        i, _, x = state
        e = eye - exact(a, x)
        return i + 1, jnp.sum(e * e), x + exact(x, e)

    _, _, x = lax.while_loop(
        lambda s: (s[0] == 0) | ((s[1] > 1e-7) & (s[0] < 4)), refine, (jnp.int32(0), jnp.float32(1.0), x)
    )
    high, mid, low = terms(x)
    z1, z2, z3 = terms(dot(low, fresh) + dot(mid, fresh) + dot(high, fresh))
    adapter = (dot(old, z3, TN) + dot(old, z2, TN) + dot(old, z1, TN)).astype(BF)
    out_ref[...] = dot(bank_ref[...], adapter).astype(BF)


def shift(x, move):
    perm = []
    for i in range(256):
        zh, y, xx, zl, c = i // 128, i // 32 % 4, i // 8 % 4, i // 2 % 4, i % 2
        zh, y, xx, zl, c = move(zh, y, xx, zl, c)
        perm.append((i, (((zh % 2) * 4 + y % 4) * 4 + xx % 4) * 8 + (zl % 4) * 2 + c % 2))
    return lax.ppermute(x, ("grp", "dev"), perm)


def along_y(x, k):
    return shift(x, lambda zh, y, xx, zl, c: (zh, y + k, xx, zl, c)) if k % 4 else x


def along_x(x, k):
    return shift(x, lambda zh, y, xx, zl, c: (zh, y, xx + k, zl, c)) if k % 4 else x


def other_core(x):
    return shift(x, lambda zh, y, xx, zl, c: (zh, y, xx, zl, c + 1))


def mirror(x):
    return shift(x, lambda zh, y, xx, zl, c: (zh + 1, y, xx, 3 - zl, c))


def local(hidden_in, w_query, w_keyval, w_out, ln_gain, ln_bias, bank, owner, slot):
    hidden = hidden_in[0]
    grp, dev = lax.axis_index("grp"), lax.axis_index("dev")
    zh, y, x, zl, c = grp // 4, grp % 4, dev // 8, dev // 2 % 4, dev % 2
    where = jnp.stack([zh, y, x, c, owner[0], slot[0], grp * 32 + dev])

    h1, h3 = along_x(hidden, 1), along_x(hidden, 3)
    h2, h2b = along_x(h1[:128], 1), along_x(h3[128:], 3)

    place = (((zh * 4 + zl) * 4 + y) * 2 + c) * 4 + x
    lane = lax.broadcasted_iota(jnp.int32, (PLACES, 1, 128), 2)
    info = jnp.where(lane == 0, where[4], jnp.where(lane == 1, where[5], place)).astype(F32)
    info = lax.all_to_all(info, ("grp", "dev"), split_axis=0, concat_axis=0, tiled=True).reshape(PLACES, 128)
    rows = call(pick_kernel, shape((PLACES, WIDTH), BF), 2**27, info, bank, where=where)

    own = call(cut_kernel, shape((CUT, 3 * CUT), BF), 2**10, w_query, w_keyval, where=where)
    out1 = shift(w_out, lambda zh, y, xx, zl, c: (c, xx, y, zl if c == zh else 3 - zl, zh))
    own = after(jnp.concatenate([own, mirror(own)], axis=0), h1, h3)
    out2 = other_core(out1)
    near = [along_y(own, k) for k in range(4)]
    near[0] = after(near[0], *near[1:], out1, h2, h2b)
    far = [other_core(w) for w in near]

    rows = exchange(after(rows, *near[1:]).reshape(64, 4, WIDTH), 2)

    part = call(
        encode_kernel,
        shape((4, WIDTH), F32),
        2**30,
        hidden,
        h1,
        h2,
        h2b,
        h3,
        *near,
        *far,
        out1,
        out2,
        where=where,
        scratch=[pltpu.VMEM((WIDTH, 6 * CUT), BF)],
        mib=24,
    )
    both = call(pack_kernel, shape((8, WIDTH), F32), 2**18, part, rows)
    both = [along_x(both, k) for k in range(4)]
    mine = call(
        norm_kernel, shape((8, WIDTH), BF), 2**14, *both, ln_gain.reshape(1, -1), ln_bias.reshape(1, -1)
    )
    here = spread(mine, 1)
    there = other_core(here)
    return call(
        update_kernel,
        shape(bank.shape, BF),
        2**31,
        here.reshape(256, WIDTH),
        there.reshape(256, WIDTH),
        bank,
        mib=32,
    )


def solution(mesh):
    in_specs = (
        P(("grp", "dev"), None, None),
        P("grp", None),
        P("grp", None),
        P("grp", None),
        P(),
        P(),
        P(("grp", "dev"), None),
        P(("grp", "dev")),
        P(("grp", "dev")),
    )
    out_specs = P(("grp", "dev"), None)
    return jax.shard_map(local, mesh=mesh, in_specs=in_specs, out_specs=out_specs, check_vma=False)
```

```python
import jax
import jax.numpy as jnp
from jax import lax
from jax.experimental import pallas as pl
from jax.experimental.pallas import tpu as pltpu
from jax.sharding import PartitionSpec as P

HEAD = 64
WIDTH = 1024
CUT = 128
PLACES = 256
BF = jnp.bfloat16
F32 = jnp.float32
NT = (((1,), (1,)), ((), ()))
TN = (((0,), (0,)), ((), ()))


def columns(cores):
    return [
        [(zh * 4 + y) * 32 + x * 8 + zl * 2 + c for zh in range(2) for zl in range(4) for y in range(4) for c in cs]
        for x in range(4)
        for cs in ([(0, 1)] if cores == 2 else [(0,), (1,)])
    ]


def exchange(x, cores):
    return lax.all_to_all(
        x, ("grp", "dev"), split_axis=0, concat_axis=0, tiled=True, axis_index_groups=columns(cores)
    )


def spread(x, cores):
    return exchange(jnp.broadcast_to(x[None], (32 * cores, *x.shape)), cores)


def after(x, *others):
    return lax.optimization_barrier((x, *others))[0]


def call(kernel, out, flops, *args, where=None, scratch=(), hbm=(), mib=12):
    vmem = pl.BlockSpec(memory_space=pltpu.VMEM)
    first = [] if where is None else [where]
    return pl.pallas_call(
        kernel,
        out_shape=out,
        in_specs=[pl.BlockSpec(memory_space=pltpu.SMEM)] * len(first)
        + [pl.BlockSpec(memory_space=pltpu.HBM) if i in hbm else vmem for i in range(len(args))],
        out_specs=jax.tree.map(lambda _: vmem, out),
        scratch_shapes=list(scratch),
        compiler_params=pltpu.CompilerParams(vmem_limit_bytes=mib * 2**20),
        cost_estimate=pl.CostEstimate(flops=flops, bytes_accessed=2**20, transcendentals=0),
    )(*first, *args)


def shape(dims, kind):
    return jax.ShapeDtypeStruct(dims, kind)


def dot(a, b, dims=(((1,), (0,)), ((), ()))):
    return lax.dot_general(a, b, dims, preferred_element_type=F32)


def exact(a, b):
    return jnp.dot(a, b, preferred_element_type=F32, precision=lax.Precision.HIGHEST)


def terms(x):
    high = x.astype(BF)
    rest = x - high.astype(F32)
    mid = rest.astype(BF)
    return high, mid, (rest - mid.astype(F32)).astype(BF)


def head_mask(rows):
    row = lax.broadcasted_iota(jnp.int32, (rows, 4 * HEAD), 0)
    col = lax.broadcasted_iota(jnp.int32, (rows, 4 * HEAD), 1)
    return lax.rem(row, 4) == lax.div(col, HEAD)


def cut_kernel(where, query_ref, keyval_ref, own_ref):
    block = 4 * where[3] + where[2]
    at = pl.ds(pl.multiple_of(block * CUT, CUT), CUT)
    own_ref[:, :CUT] = query_ref[:, at]
    own_ref[:, CUT : 2 * CUT] = keyval_ref[:, at]
    own_ref[:, 2 * CUT :] = keyval_ref[:, pl.ds(pl.multiple_of(block * CUT + WIDTH, CUT), CUT)]


def pick_kernel(where, info_ref, bank_ref, rows_ref):
    n = bank_ref.shape[0]
    number = lax.broadcasted_iota(jnp.int32, (PLACES, n), 1).astype(F32)
    own, slot, place = [info_ref[:, i : i + 1] for i in range(3)]
    a = jnp.where((place == number) & (own == where[6].astype(F32)), 1.0, 0.0).astype(BF)
    b = jnp.where(slot == number, 1.0, 0.0).astype(BF)
    rows_ref[...] = dot(dot(a, b, TN).astype(BF), bank_ref[...]).astype(BF)


def row_blocks(where):
    zh, y = where[0], where[1]
    for k in range(4):
        yk = lax.rem(y + 4 - k, 4)
        for h in range(2):
            at = ((zh if h == 0 else 1 - zh) * 4 + yk) * CUT
            yield k, slice(h * CUT, (h + 1) * CUT), pl.ds(pl.multiple_of(at, CUT), CUT)


def encode_kernel(
    where, h0, h1, h2, h2b, h3, n0, n1, n2, n3, f0, f1, f2, f3, out_ref, out2_ref, part_ref, w_ref
):
    near, far = (n0, n1, n2, n3), (f0, f1, f2, f3)
    for k, rows, features in row_blocks(where):
        for i in range(3):
            cols = slice(i * CUT, (i + 1) * CUT)
            w_ref[features, 2 * i * CUT : (2 * i + 1) * CUT] = near[k][rows, cols]
            w_ref[features, (2 * i + 1) * CUT : (2 * i + 2) * CUT] = far[k][rows, cols]
    four = 4 * HEAD
    mask = head_mask(4)
    contexts = []
    for refs in ((h0,), (h1,), (h2, h2b), (h3,)):
        x = jnp.concatenate([r[...] for r in refs], axis=0)
        keyval = dot(x, w_ref[:, four:]).astype(BF)
        query = (0.125 * dot(x[0:16], w_ref[:, :four])[0:1]).astype(BF).astype(F32)
        query = jnp.where(mask, jnp.broadcast_to(query, (4, four)), 0.0).astype(BF)
        scores = dot(query, keyval[:, :four], NT)
        e = jnp.exp(scores - jnp.max(scores, axis=1, keepdims=True))
        probs = (e / jnp.sum(e, axis=1, keepdims=True)).astype(BF)
        context = jnp.where(mask, dot(probs, keyval[:, four:]), 0.0)
        contexts.append(jnp.sum(context, axis=0, keepdims=True))
    context = jnp.concatenate(contexts, axis=0).astype(BF)
    part = dot(context[:, :CUT], out_ref[...]) + dot(context[:, CUT:], out2_ref[...])
    for k in range(4):
        row = part[k : k + 1]
        if k == 0:
            row = row + h0[0:1, :].astype(F32)
        part_ref[pl.ds(lax.rem(where[2] + 4 - k, 4), 1), :] = row


def pack_kernel(part_ref, old_ref, both_ref):
    both_ref[...] = jnp.concatenate([part_ref[...], jnp.sum(old_ref[...].astype(F32), axis=0)], axis=0)


def norm_kernel(t0, t1, t2, t3, gain_ref, bias_ref, rows_ref):
    total = (t0[...] + t1[...]) + (t2[...] + t3[...])
    joined = total[0:4]
    center = joined - jnp.mean(joined, axis=-1, keepdims=True)
    var = jnp.mean(center * center, axis=-1, keepdims=True)
    normed = center / jnp.sqrt(var + 1e-05) * gain_ref[...] + bias_ref[...]
    fresh = normed / jnp.sqrt(jnp.mean(normed * normed, axis=-1, keepdims=True) + 1e-06)
    rows_ref[...] = jnp.concatenate([fresh, total[4:8]], axis=0).astype(BF)


def product(a, b):
    a1, a2, _ = terms(a)
    b1, b2, _ = terms(b)
    return dot(a2, b1) + dot(a1, b2) + dot(a1, b1)


def update_kernel(here_ref, there_ref, bank_ref, out_ref):
    half = here_ref.shape[0] // 2
    row = lax.broadcasted_iota(jnp.int32, (half, 2 * half), 0)
    col = lax.broadcasted_iota(jnp.int32, (half, 2 * half), 1)
    at = lax.div(row, 4) * 8 + lax.rem(row, 4)

    def take(first):
        pick = jnp.where(col == at + first, 1.0, 0.0).astype(BF)
        return jnp.concatenate([dot(pick, ref[...]).astype(BF) for ref in (here_ref, there_ref)], axis=0)

    old, fresh = take(4), take(0)
    n = 2 * half
    rows = lax.broadcasted_iota(jnp.int32, (n, n), 0)
    cols = lax.broadcasted_iota(jnp.int32, (n, n), 1)
    eye = jnp.where(rows == cols, 1.0, 0.0).astype(F32)
    ridge = 0.25 * n
    a = dot(old, old, NT) + ridge * eye
    norm = jnp.max(jnp.sum(jnp.abs(a), axis=1, keepdims=True))
    c = 2.0 / (ridge + norm)
    r = eye - c * a
    x = c * (eye + r)

    def size(r):
        return jnp.max(jnp.sum(jnp.abs(r), axis=1, keepdims=True))

    def step(times, state):
        t, _, x, r = state
        both = times(jnp.concatenate([x, r], axis=0), r)
        r = both[n:]
        return 2.0 * t, size(r), x + both[:n], r

    def more(state):
        return (state[0] < 9.0) & (state[1] > 1e-4)

    r = exact(r, r)
    state = (2.0 * c * ridge, size(r), x, r)
    state = lax.while_loop(lambda s: more(s) & (norm < 512.0 * ridge), lambda s: step(product, s), state)
    x = lax.while_loop(more, lambda s: step(exact, s), state)[2]

    def refine(state):
        i, _, x = state
        e = eye - exact(a, x)
        return i + 1, jnp.sum(e * e), x + exact(x, e)

    _, _, x = lax.while_loop(
        lambda s: (s[0] == 0) | ((s[1] > 1e-7) & (s[0] < 4)), refine, (jnp.int32(0), jnp.float32(1.0), x)
    )
    high, mid, low = terms(x)
    z1, z2, z3 = terms(dot(low, fresh) + dot(mid, fresh) + dot(high, fresh))
    adapter = (dot(old, z3, TN) + dot(old, z2, TN) + dot(old, z1, TN)).astype(BF)
    out_ref[...] = dot(bank_ref[...], adapter).astype(BF)


def shift(x, move):
    perm = []
    for i in range(256):
        zh, y, xx, zl, c = i // 128, i // 32 % 4, i // 8 % 4, i // 2 % 4, i % 2
        zh, y, xx, zl, c = move(zh, y, xx, zl, c)
        perm.append((i, (((zh % 2) * 4 + y % 4) * 4 + xx % 4) * 8 + (zl % 4) * 2 + c % 2))
    return lax.ppermute(x, ("grp", "dev"), perm)


def along_y(x, k):
    return shift(x, lambda zh, y, xx, zl, c: (zh, y + k, xx, zl, c)) if k % 4 else x


def along_x(x, k):
    return shift(x, lambda zh, y, xx, zl, c: (zh, y, xx + k, zl, c)) if k % 4 else x


def other_core(x):
    return shift(x, lambda zh, y, xx, zl, c: (zh, y, xx, zl, c + 1))


def mirror(x):
    return shift(x, lambda zh, y, xx, zl, c: (zh + 1, y, xx, 3 - zl, c))


def local(hidden_in, w_query, w_keyval, w_out, ln_gain, ln_bias, bank, owner, slot):
    hidden = hidden_in[0]
    grp, dev = lax.axis_index("grp"), lax.axis_index("dev")
    zh, y, x, zl, c = grp // 4, grp % 4, dev // 8, dev // 2 % 4, dev % 2
    where = jnp.stack([zh, y, x, c, owner[0], slot[0], grp * 32 + dev])

    h1, h3 = along_x(hidden, 1), along_x(hidden, 3)
    h2, h2b = along_x(h1[:128], 1), along_x(h3[128:], 3)

    place = (((zh * 4 + zl) * 4 + y) * 2 + c) * 4 + x
    lane = lax.broadcasted_iota(jnp.int32, (PLACES, 1, 128), 2)
    info = jnp.where(lane == 0, where[4], jnp.where(lane == 1, where[5], place)).astype(F32)
    info = lax.all_to_all(info, ("grp", "dev"), split_axis=0, concat_axis=0, tiled=True).reshape(PLACES, 128)
    rows = call(pick_kernel, shape((PLACES, WIDTH), BF), 2**27, info, bank, where=where)

    own = call(cut_kernel, shape((CUT, 3 * CUT), BF), 2**10, w_query, w_keyval, where=where)
    out1 = shift(w_out, lambda zh, y, xx, zl, c: (c, xx, y, zl if c == zh else 3 - zl, zh))
    own = after(jnp.concatenate([own, mirror(own)], axis=0), h1, h3)
    out2 = other_core(out1)
    near = [along_y(own, k) for k in range(4)]
    near[0] = after(near[0], *near[1:], out1, h2, h2b)
    far = [other_core(w) for w in near]

    rows = exchange(after(rows, *near[1:], out1, h2, h2b).reshape(64, 4, WIDTH), 2)

    part = call(
        encode_kernel,
        shape((4, WIDTH), F32),
        2**30,
        hidden,
        h1,
        h2,
        h2b,
        h3,
        *near,
        *far,
        out1,
        out2,
        where=where,
        scratch=[pltpu.VMEM((WIDTH, 6 * CUT), BF)],
        mib=24,
    )
    both = call(pack_kernel, shape((8, WIDTH), F32), 2**18, part, rows)
    both = [along_x(both, k) for k in range(4)]
    mine = call(
        norm_kernel, shape((8, WIDTH), BF), 2**14, *both, ln_gain.reshape(1, -1), ln_bias.reshape(1, -1)
    )
    here = spread(mine, 1)
    there = other_core(here)
    return call(
        update_kernel,
        shape(bank.shape, BF),
        2**31,
        here.reshape(256, WIDTH),
        there.reshape(256, WIDTH),
        bank,
        mib=32,
    )


def solution(mesh):
    in_specs = (
        P(("grp", "dev"), None, None),
        P("grp", None),
        P("grp", None),
        P("grp", None),
        P(),
        P(),
        P(("grp", "dev"), None),
        P(("grp", "dev")),
        P(("grp", "dev")),
    )
    out_specs = P(("grp", "dev"), None)
    return jax.shard_map(local, mesh=mesh, in_specs=in_specs, out_specs=out_specs, check_vma=False)
```

```python
import jax
import jax.numpy as jnp
from jax import lax
from jax.experimental import pallas as pl
from jax.experimental.pallas import tpu as pltpu
from jax.sharding import PartitionSpec as P

HEAD = 64
WIDTH = 1024
CUT = 128
PLACES = 256
BF = jnp.bfloat16
F32 = jnp.float32
NT = (((1,), (1,)), ((), ()))
TN = (((0,), (0,)), ((), ()))


def columns(cores):
    return [
        [(zh * 4 + y) * 32 + x * 8 + zl * 2 + c for zh in range(2) for zl in range(4) for y in range(4) for c in cs]
        for x in range(4)
        for cs in ([(0, 1)] if cores == 2 else [(0,), (1,)])
    ]


def exchange(x, cores):
    return lax.all_to_all(
        x, ("grp", "dev"), split_axis=0, concat_axis=0, tiled=True, axis_index_groups=columns(cores)
    )


def spread(x, cores):
    return exchange(jnp.broadcast_to(x[None], (32 * cores, *x.shape)), cores)


def after(x, *others):
    return lax.optimization_barrier((x, *others))[0]


def call(kernel, out, flops, *args, where=None, scratch=(), hbm=(), mib=12):
    vmem = pl.BlockSpec(memory_space=pltpu.VMEM)
    first = [] if where is None else [where]
    return pl.pallas_call(
        kernel,
        out_shape=out,
        in_specs=[pl.BlockSpec(memory_space=pltpu.SMEM)] * len(first)
        + [pl.BlockSpec(memory_space=pltpu.HBM) if i in hbm else vmem for i in range(len(args))],
        out_specs=jax.tree.map(lambda _: vmem, out),
        scratch_shapes=list(scratch),
        compiler_params=pltpu.CompilerParams(vmem_limit_bytes=mib * 2**20),
        cost_estimate=pl.CostEstimate(flops=flops, bytes_accessed=2**20, transcendentals=0),
    )(*first, *args)


def shape(dims, kind):
    return jax.ShapeDtypeStruct(dims, kind)


def dot(a, b, dims=(((1,), (0,)), ((), ()))):
    return lax.dot_general(a, b, dims, preferred_element_type=F32)


def exact(a, b):
    return jnp.dot(a, b, preferred_element_type=F32, precision=lax.Precision.HIGHEST)


def terms(x):
    high = x.astype(BF)
    rest = x - high.astype(F32)
    mid = rest.astype(BF)
    return high, mid, (rest - mid.astype(F32)).astype(BF)


def head_mask(rows):
    row = lax.broadcasted_iota(jnp.int32, (rows, 4 * HEAD), 0)
    col = lax.broadcasted_iota(jnp.int32, (rows, 4 * HEAD), 1)
    return lax.rem(row, 4) == lax.div(col, HEAD)


def cut_kernel(where, query_ref, keyval_ref, own_ref):
    block = 4 * where[3] + where[2]
    at = pl.ds(pl.multiple_of(block * CUT, CUT), CUT)
    own_ref[:, :CUT] = query_ref[:, at]
    own_ref[:, CUT : 2 * CUT] = keyval_ref[:, at]
    own_ref[:, 2 * CUT :] = keyval_ref[:, pl.ds(pl.multiple_of(block * CUT + WIDTH, CUT), CUT)]


def pick_kernel(where, info_ref, bank_ref, keep_ref, give_ref, select_ref):
    n = bank_ref.shape[0]
    number = lax.broadcasted_iota(jnp.int32, (PLACES, n), 1).astype(F32)
    own, slot, place = [info_ref[:, i : i + 1] for i in range(3)]
    a = jnp.where((place == number) & (own == where[6].astype(F32)), 1.0, 0.0).astype(BF)
    b = jnp.where(slot == number, 1.0, 0.0).astype(BF)
    select_ref[...] = dot(a, b, TN)
    for ref, c in ((keep_ref, where[3]), (give_ref, 1 - where[3])):
        half = pl.ds(pl.multiple_of(c * (PLACES // 2), PLACES // 2), PLACES // 2)
        ref[...] = dot(select_ref[half, :].astype(BF), bank_ref[...]).astype(BF)


def row_blocks(where):
    zh, y = where[0], where[1]
    for k in range(4):
        yk = lax.rem(y + 4 - k, 4)
        for h in range(2):
            at = ((zh if h == 0 else 1 - zh) * 4 + yk) * CUT
            yield k, slice(h * CUT, (h + 1) * CUT), pl.ds(pl.multiple_of(at, CUT), CUT)


def encode_kernel(
    where, h0, h1, h2, h3, n0, n1, n2, n3, f0, f1, f2, f3, out_ref, out2_ref, part_ref, w_ref
):
    near, far = (n0, n1, n2, n3), (f0, f1, f2, f3)
    for k, rows, features in row_blocks(where):
        for i in range(3):
            cols = slice(i * CUT, (i + 1) * CUT)
            w_ref[features, 2 * i * CUT : (2 * i + 1) * CUT] = near[k][rows, cols]
            w_ref[features, (2 * i + 1) * CUT : (2 * i + 2) * CUT] = far[k][rows, cols]
    four = 4 * HEAD
    mask = head_mask(4)
    contexts = []
    for ref in (h0, h1, h2, h3):
        x = ref[...]
        keyval = dot(x, w_ref[:, four:]).astype(BF)
        query = (0.125 * dot(x[0:16], w_ref[:, :four])[0:1]).astype(BF).astype(F32)
        query = jnp.where(mask, jnp.broadcast_to(query, (4, four)), 0.0).astype(BF)
        scores = dot(query, keyval[:, :four], NT)
        e = jnp.exp(scores - jnp.max(scores, axis=1, keepdims=True))
        probs = (e / jnp.sum(e, axis=1, keepdims=True)).astype(BF)
        context = jnp.where(mask, dot(probs, keyval[:, four:]), 0.0)
        contexts.append(jnp.sum(context, axis=0, keepdims=True))
    context = jnp.concatenate(contexts, axis=0).astype(BF)
    part = dot(context[:, :CUT], out_ref[...]) + dot(context[:, CUT:], out2_ref[...])
    for k in range(4):
        row = part[k : k + 1]
        if k == 0:
            row = row + h0[0:1, :].astype(F32)
        part_ref[pl.ds(lax.rem(where[2] + 4 - k, 4), 1), :] = row


def pack_kernel(part_ref, old_ref, both_ref):
    both_ref[...] = jnp.concatenate([part_ref[...], jnp.sum(old_ref[...].astype(F32), axis=0)], axis=0)


def norm_kernel(t0, t1, t2, t3, gain_ref, bias_ref, rows_ref):
    total = (t0[...] + t1[...]) + (t2[...] + t3[...])
    joined = total[0:4]
    center = joined - jnp.mean(joined, axis=-1, keepdims=True)
    var = jnp.mean(center * center, axis=-1, keepdims=True)
    normed = center / jnp.sqrt(var + 1e-05) * gain_ref[...] + bias_ref[...]
    fresh = normed / jnp.sqrt(jnp.mean(normed * normed, axis=-1, keepdims=True) + 1e-06)
    rows_ref[...] = jnp.concatenate([fresh, total[4:8]], axis=0).astype(BF)


def product(a, b):
    a1, a2, _ = terms(a)
    b1, b2, _ = terms(b)
    return dot(a2, b1) + dot(a1, b2) + dot(a1, b1)


def update_kernel(here_ref, there_ref, bank_ref, out_ref):
    half = here_ref.shape[0] // 2
    row = lax.broadcasted_iota(jnp.int32, (half, 2 * half), 0)
    col = lax.broadcasted_iota(jnp.int32, (half, 2 * half), 1)
    at = lax.div(row, 4) * 8 + lax.rem(row, 4)

    def take(first):
        pick = jnp.where(col == at + first, 1.0, 0.0).astype(BF)
        return jnp.concatenate([dot(pick, ref[...]).astype(BF) for ref in (here_ref, there_ref)], axis=0)

    old, fresh = take(4), take(0)
    n = 2 * half
    rows = lax.broadcasted_iota(jnp.int32, (n, n), 0)
    cols = lax.broadcasted_iota(jnp.int32, (n, n), 1)
    eye = jnp.where(rows == cols, 1.0, 0.0).astype(F32)
    ridge = 0.25 * n
    a = dot(old, old, NT) + ridge * eye
    norm = jnp.max(jnp.sum(jnp.abs(a), axis=1, keepdims=True))
    c = 2.0 / (ridge + norm)
    r = eye - c * a
    x = c * (eye + r)

    def size(r):
        return jnp.max(jnp.sum(jnp.abs(r), axis=1, keepdims=True))

    def step(times, state):
        t, _, x, r = state
        both = times(jnp.concatenate([x, r], axis=0), r)
        r = both[n:]
        return 2.0 * t, size(r), x + both[:n], r

    def more(state):
        return (state[0] < 9.0) & (state[1] > 1e-4)

    r = exact(r, r)
    state = (2.0 * c * ridge, size(r), x, r)
    state = lax.while_loop(lambda s: more(s) & (norm < 512.0 * ridge), lambda s: step(product, s), state)
    x = lax.while_loop(more, lambda s: step(exact, s), state)[2]

    def refine(state):
        i, _, x = state
        e = eye - exact(a, x)
        return i + 1, jnp.sum(e * e), x + exact(x, e)

    _, _, x = lax.while_loop(
        lambda s: (s[0] == 0) | ((s[1] > 1e-7) & (s[0] < 4)), refine, (jnp.int32(0), jnp.float32(1.0), x)
    )
    high, mid, low = terms(x)
    z1, z2, z3 = terms(dot(low, fresh) + dot(mid, fresh) + dot(high, fresh))
    adapter = (dot(old, z3, TN) + dot(old, z2, TN) + dot(old, z1, TN)).astype(BF)
    out_ref[...] = dot(bank_ref[...], adapter).astype(BF)


def shift(x, move):
    perm = []
    for i in range(256):
        zh, y, xx, zl, c = i // 128, i // 32 % 4, i // 8 % 4, i // 2 % 4, i % 2
        zh, y, xx, zl, c = move(zh, y, xx, zl, c)
        perm.append((i, (((zh % 2) * 4 + y % 4) * 4 + xx % 4) * 8 + (zl % 4) * 2 + c % 2))
    return lax.ppermute(x, ("grp", "dev"), perm)


def along_y(x, k):
    return shift(x, lambda zh, y, xx, zl, c: (zh, y + k, xx, zl, c)) if k % 4 else x


def along_x(x, k):
    return shift(x, lambda zh, y, xx, zl, c: (zh, y, xx + k, zl, c)) if k % 4 else x


def other_core(x):
    return shift(x, lambda zh, y, xx, zl, c: (zh, y, xx, zl, c + 1))


def mirror(x):
    return shift(x, lambda zh, y, xx, zl, c: (zh + 1, y, xx, 3 - zl, c))


def local(hidden_in, w_query, w_keyval, w_out, ln_gain, ln_bias, bank, owner, slot):
    hidden = hidden_in[0]
    grp, dev = lax.axis_index("grp"), lax.axis_index("dev")
    zh, y, x, zl, c = grp // 4, grp % 4, dev // 8, dev // 2 % 4, dev % 2
    where = jnp.stack([zh, y, x, c, owner[0], slot[0], grp * 32 + dev])

    h1, h3 = along_x(hidden, 1), along_x(hidden, 3)
    h2 = along_x(h1, 1)

    own = call(cut_kernel, shape((CUT, 3 * CUT), BF), 2**10, w_query, w_keyval, where=where)
    out1 = shift(w_out, lambda zh, y, xx, zl, c: (c, xx, y, zl if c == zh else 3 - zl, zh))
    got = mirror(own)
    own = after(jnp.concatenate([own, got], axis=0), h1, h3)
    out2 = other_core(out1)
    near = [along_y(own, k) for k in range(4)]
    near[0] = after(near[0], *near[1:], out1, h2)
    far = [other_core(w) for w in near]

    place = (((c * 2 + zh) * 4 + zl) * 4 + y) * 4 + x
    lane = lax.broadcasted_iota(jnp.int32, (PLACES, 1, 128), 2)
    info = jnp.where(lane == 0, where[4], jnp.where(lane == 1, where[5], place)).astype(F32)
    info = lax.all_to_all(after(info, got), ("grp", "dev"), split_axis=0, concat_axis=0, tiled=True).reshape(PLACES, 128)
    half = shape((PLACES // 2, WIDTH), BF)
    keep, give = call(
        pick_kernel, [half, half], 2**27, info, bank, where=where, scratch=[pltpu.VMEM((PLACES, PLACES), F32)]
    )
    rows = keep + other_core(after(give, *near[1:]))
    rows = exchange(after(rows, *far, out2).reshape(32, 4, WIDTH), 1)

    part = call(
        encode_kernel,
        shape((4, WIDTH), F32),
        2**30,
        hidden,
        h1,
        h2,
        h3,
        *near,
        *far,
        out1,
        out2,
        where=where,
        scratch=[pltpu.VMEM((WIDTH, 6 * CUT), BF)],
    )
    both = call(pack_kernel, shape((8, WIDTH), F32), 2**18, part, rows)
    both = [along_x(both, k) for k in range(4)]
    mine = call(
        norm_kernel, shape((8, WIDTH), BF), 2**14, *both, ln_gain.reshape(1, -1), ln_bias.reshape(1, -1)
    )
    here = spread(mine, 1)
    there = other_core(here)
    return call(
        update_kernel,
        shape(bank.shape, BF),
        2**31,
        here.reshape(256, WIDTH),
        there.reshape(256, WIDTH),
        bank,
        mib=24,
    )


def solution(mesh):
    in_specs = (
        P(("grp", "dev"), None, None),
        P("grp", None),
        P("grp", None),
        P("grp", None),
        P(),
        P(),
        P(("grp", "dev"), None),
        P(("grp", "dev")),
        P(("grp", "dev")),
    )
    out_specs = P(("grp", "dev"), None)
    return jax.shard_map(local, mesh=mesh, in_specs=in_specs, out_specs=out_specs, check_vma=False)
```

```python
import jax
import jax.numpy as jnp
from jax import lax
from jax.experimental import pallas as pl
from jax.experimental.pallas import tpu as pltpu
from jax.sharding import PartitionSpec as P

HEAD = 64
WIDTH = 1024
CUT = 128
PLACES = 256
BF = jnp.bfloat16
F32 = jnp.float32
NT = (((1,), (1,)), ((), ()))
TN = (((0,), (0,)), ((), ()))


def columns(cores):
    return [
        [(zh * 4 + y) * 32 + x * 8 + zl * 2 + c for zh in range(2) for zl in range(4) for y in range(4) for c in cs]
        for x in range(4)
        for cs in ([(0, 1)] if cores == 2 else [(0,), (1,)])
    ]


def exchange(x, cores):
    return lax.all_to_all(
        x, ("grp", "dev"), split_axis=0, concat_axis=0, tiled=True, axis_index_groups=columns(cores)
    )


def spread(x, cores):
    return exchange(jnp.broadcast_to(x[None], (32 * cores, *x.shape)), cores)


def after(x, *others):
    return lax.optimization_barrier((x, *others))[0]


def call(kernel, out, flops, *args, where=None, scratch=(), hbm=(), mib=12):
    vmem = pl.BlockSpec(memory_space=pltpu.VMEM)
    first = [] if where is None else [where]
    return pl.pallas_call(
        kernel,
        out_shape=out,
        in_specs=[pl.BlockSpec(memory_space=pltpu.SMEM)] * len(first)
        + [pl.BlockSpec(memory_space=pltpu.HBM) if i in hbm else vmem for i in range(len(args))],
        out_specs=jax.tree.map(lambda _: vmem, out),
        scratch_shapes=list(scratch),
        compiler_params=pltpu.CompilerParams(vmem_limit_bytes=mib * 2**20),
        cost_estimate=pl.CostEstimate(flops=flops, bytes_accessed=2**20, transcendentals=0),
    )(*first, *args)


def shape(dims, kind):
    return jax.ShapeDtypeStruct(dims, kind)


def dot(a, b, dims=(((1,), (0,)), ((), ()))):
    return lax.dot_general(a, b, dims, preferred_element_type=F32)


def exact(a, b):
    return jnp.dot(a, b, preferred_element_type=F32, precision=lax.Precision.HIGHEST)


def terms(x):
    high = x.astype(BF)
    rest = x - high.astype(F32)
    mid = rest.astype(BF)
    return high, mid, (rest - mid.astype(F32)).astype(BF)


def head_mask(rows):
    row = lax.broadcasted_iota(jnp.int32, (rows, 4 * HEAD), 0)
    col = lax.broadcasted_iota(jnp.int32, (rows, 4 * HEAD), 1)
    return lax.rem(row, 4) == lax.div(col, HEAD)


def cut_kernel(where, query_ref, keyval_ref, own_ref):
    block = 4 * where[3] + where[2]
    at = pl.ds(pl.multiple_of(block * CUT, CUT), CUT)
    own_ref[:, :CUT] = query_ref[:, at]
    own_ref[:, CUT : 2 * CUT] = keyval_ref[:, at]
    own_ref[:, 2 * CUT :] = keyval_ref[:, pl.ds(pl.multiple_of(block * CUT + WIDTH, CUT), CUT)]


def pick_kernel(where, info_ref, bank_ref, keep_ref, give_ref, select_ref):
    n = bank_ref.shape[0]
    number = lax.broadcasted_iota(jnp.int32, (PLACES, n), 1).astype(F32)
    own, slot, place = [info_ref[:, i : i + 1] for i in range(3)]
    a = jnp.where((place == number) & (own == where[6].astype(F32)), 1.0, 0.0).astype(BF)
    b = jnp.where(slot == number, 1.0, 0.0).astype(BF)
    select_ref[...] = dot(a, b, TN)
    for ref, c in ((keep_ref, where[3]), (give_ref, 1 - where[3])):
        half = pl.ds(pl.multiple_of(c * (PLACES // 2), PLACES // 2), PLACES // 2)
        ref[...] = dot(select_ref[half, :].astype(BF), bank_ref[...]).astype(BF)


def row_blocks(where):
    zh, y = where[0], where[1]
    for k in range(4):
        yk = lax.rem(y + 4 - k, 4)
        for h in range(2):
            at = ((zh if h == 0 else 1 - zh) * 4 + yk) * CUT
            yield k, slice(h * CUT, (h + 1) * CUT), pl.ds(pl.multiple_of(at, CUT), CUT)


def encode_kernel(
    where, h0, h1, h2, h3, n0, n1, n2, n3, f0, f1, f2, f3, out_ref, out2_ref, part_ref, w_ref
):
    near, far = (n0, n1, n2, n3), (f0, f1, f2, f3)
    for k, rows, features in row_blocks(where):
        for i in range(3):
            cols = slice(i * CUT, (i + 1) * CUT)
            w_ref[features, 2 * i * CUT : (2 * i + 1) * CUT] = near[k][rows, cols]
            w_ref[features, (2 * i + 1) * CUT : (2 * i + 2) * CUT] = far[k][rows, cols]
    four = 4 * HEAD
    mask = head_mask(4)
    contexts = []
    for ref in (h0, h1, h2, h3):
        x = ref[...]
        keyval = dot(x, w_ref[:, four:]).astype(BF)
        query = (0.125 * dot(x[0:16], w_ref[:, :four])[0:1]).astype(BF).astype(F32)
        query = jnp.where(mask, jnp.broadcast_to(query, (4, four)), 0.0).astype(BF)
        scores = dot(query, keyval[:, :four], NT)
        e = jnp.exp(scores - jnp.max(scores, axis=1, keepdims=True))
        probs = (e / jnp.sum(e, axis=1, keepdims=True)).astype(BF)
        context = jnp.where(mask, dot(probs, keyval[:, four:]), 0.0)
        contexts.append(jnp.sum(context, axis=0, keepdims=True))
    context = jnp.concatenate(contexts, axis=0).astype(BF)
    part = dot(context[:, :CUT], out_ref[...]) + dot(context[:, CUT:], out2_ref[...])
    for k in range(4):
        row = part[k : k + 1]
        if k == 0:
            row = row + h0[0:1, :].astype(F32)
        part_ref[pl.ds(lax.rem(where[2] + 4 - k, 4), 1), :] = row


def pack_kernel(part_ref, old_ref, both_ref):
    both_ref[...] = jnp.concatenate([part_ref[...], jnp.sum(old_ref[...].astype(F32), axis=0)], axis=0)


def norm_kernel(t0, t1, t2, t3, gain_ref, bias_ref, rows_ref):
    total = (t0[...] + t1[...]) + (t2[...] + t3[...])
    joined = total[0:4]
    center = joined - jnp.mean(joined, axis=-1, keepdims=True)
    var = jnp.mean(center * center, axis=-1, keepdims=True)
    normed = center / jnp.sqrt(var + 1e-05) * gain_ref[...] + bias_ref[...]
    fresh = normed / jnp.sqrt(jnp.mean(normed * normed, axis=-1, keepdims=True) + 1e-06)
    rows_ref[...] = jnp.concatenate([fresh, total[4:8]], axis=0).astype(BF)


def product(a, b):
    a1, a2, _ = terms(a)
    b1, b2, _ = terms(b)
    return dot(a2, b1) + dot(a1, b2) + dot(a1, b1)


def update_kernel(here_ref, there_ref, bank_ref, out_ref):
    half = here_ref.shape[0] // 2
    row = lax.broadcasted_iota(jnp.int32, (half, 2 * half), 0)
    col = lax.broadcasted_iota(jnp.int32, (half, 2 * half), 1)
    at = lax.div(row, 4) * 8 + lax.rem(row, 4)

    def take(first):
        pick = jnp.where(col == at + first, 1.0, 0.0).astype(BF)
        return jnp.concatenate([dot(pick, ref[...]).astype(BF) for ref in (here_ref, there_ref)], axis=0)

    old, fresh = take(4), take(0)
    n = 2 * half
    rows = lax.broadcasted_iota(jnp.int32, (n, n), 0)
    cols = lax.broadcasted_iota(jnp.int32, (n, n), 1)
    eye = jnp.where(rows == cols, 1.0, 0.0).astype(F32)
    ridge = 0.25 * n
    a = dot(old, old, NT) + ridge * eye
    norm = jnp.max(jnp.sum(jnp.abs(a), axis=1, keepdims=True))
    c = 2.0 / (ridge + norm)
    r = eye - c * a
    x = c * (eye + r)

    def size(r):
        return jnp.max(jnp.sum(jnp.abs(r), axis=1, keepdims=True))

    def step(times, state):
        t, _, x, r = state
        both = times(jnp.concatenate([x, r], axis=0), r)
        r = both[n:]
        return 2.0 * t, size(r), x + both[:n], r

    def more(state):
        return (state[0] < 9.0) & (state[1] > 1e-4)

    r = exact(r, r)
    state = (2.0 * c * ridge, size(r), x, r)
    state = lax.while_loop(lambda s: more(s) & (norm < 512.0 * ridge), lambda s: step(product, s), state)
    x = lax.while_loop(more, lambda s: step(exact, s), state)[2]

    def refine(state):
        i, _, x = state
        e = eye - exact(a, x)
        return i + 1, jnp.sum(e * e), x + exact(x, e)

    _, _, x = lax.while_loop(
        lambda s: (s[0] == 0) | ((s[1] > 1e-7) & (s[0] < 4)), refine, (jnp.int32(0), jnp.float32(1.0), x)
    )
    high, mid, low = terms(x)
    z1, z2, z3 = terms(dot(low, fresh) + dot(mid, fresh) + dot(high, fresh))
    adapter = (dot(old, z3, TN) + dot(old, z2, TN) + dot(old, z1, TN)).astype(BF)
    out_ref[...] = dot(bank_ref[...], adapter).astype(BF)


def shift(x, move):
    perm = []
    for i in range(256):
        zh, y, xx, zl, c = i // 128, i // 32 % 4, i // 8 % 4, i // 2 % 4, i % 2
        zh, y, xx, zl, c = move(zh, y, xx, zl, c)
        perm.append((i, (((zh % 2) * 4 + y % 4) * 4 + xx % 4) * 8 + (zl % 4) * 2 + c % 2))
    return lax.ppermute(x, ("grp", "dev"), perm)


def along_y(x, k):
    return shift(x, lambda zh, y, xx, zl, c: (zh, y + k, xx, zl, c)) if k % 4 else x


def along_x(x, k):
    return shift(x, lambda zh, y, xx, zl, c: (zh, y, xx + k, zl, c)) if k % 4 else x


def other_core(x):
    return shift(x, lambda zh, y, xx, zl, c: (zh, y, xx, zl, c + 1))


def mirror(x):
    return shift(x, lambda zh, y, xx, zl, c: (zh + 1, y, xx, 3 - zl, c))


def local(hidden_in, w_query, w_keyval, w_out, ln_gain, ln_bias, bank, owner, slot):
    hidden = hidden_in[0]
    grp, dev = lax.axis_index("grp"), lax.axis_index("dev")
    zh, y, x, zl, c = grp // 4, grp % 4, dev // 8, dev // 2 % 4, dev % 2
    where = jnp.stack([zh, y, x, c, owner[0], slot[0], grp * 32 + dev])

    h1, h3 = along_x(hidden, 1), along_x(hidden, 3)
    h2 = along_x(h1, 1)

    own = call(cut_kernel, shape((CUT, 3 * CUT), BF), 2**10, w_query, w_keyval, where=where)
    out1 = shift(w_out, lambda zh, y, xx, zl, c: (c, xx, y, zl if c == zh else 3 - zl, zh))
    got = mirror(own)
    own = after(jnp.concatenate([own, got], axis=0), h1, h3, out1)
    out2 = other_core(out1)
    near = [along_y(own, k) for k in range(4)]
    near[0] = after(near[0], *near[1:], h2)
    far = [other_core(w) for w in near]

    place = (((c * 2 + zh) * 4 + zl) * 4 + y) * 4 + x
    lane = lax.broadcasted_iota(jnp.int32, (PLACES, 1, 128), 2)
    info = jnp.where(lane == 0, where[4], jnp.where(lane == 1, where[5], place)).astype(F32)
    info = lax.all_to_all(after(info, got), ("grp", "dev"), split_axis=0, concat_axis=0, tiled=True).reshape(PLACES, 128)
    half = shape((PLACES // 2, WIDTH), BF)
    keep, give = call(
        pick_kernel, [half, half], 2**27, info, bank, where=where, scratch=[pltpu.VMEM((PLACES, PLACES), F32)]
    )
    rows = keep + other_core(after(give, *near[1:]))
    rows = exchange(after(rows, *near[1:], h2).reshape(32, 4, WIDTH), 1)

    part = call(
        encode_kernel,
        shape((4, WIDTH), F32),
        2**30,
        hidden,
        h1,
        h2,
        h3,
        *near,
        *far,
        out1,
        out2,
        where=where,
        scratch=[pltpu.VMEM((WIDTH, 6 * CUT), BF)],
    )
    both = call(pack_kernel, shape((8, WIDTH), F32), 2**18, part, rows)
    both = [along_x(both, k) for k in range(4)]
    mine = call(
        norm_kernel, shape((8, WIDTH), BF), 2**14, *both, ln_gain.reshape(1, -1), ln_bias.reshape(1, -1)
    )
    here = spread(mine, 1)
    there = other_core(here)
    return call(
        update_kernel,
        shape(bank.shape, BF),
        2**31,
        here.reshape(256, WIDTH),
        there.reshape(256, WIDTH),
        bank,
        mib=24,
    )


def solution(mesh):
    in_specs = (
        P(("grp", "dev"), None, None),
        P("grp", None),
        P("grp", None),
        P("grp", None),
        P(),
        P(),
        P(("grp", "dev"), None),
        P(("grp", "dev")),
        P(("grp", "dev")),
    )
    out_specs = P(("grp", "dev"), None)
    return jax.shard_map(local, mesh=mesh, in_specs=in_specs, out_specs=out_specs, check_vma=False)
```

```python
import jax
import jax.numpy as jnp
from jax import lax
from jax.experimental import pallas as pl
from jax.experimental.pallas import tpu as pltpu
from jax.sharding import PartitionSpec as P

HEAD = 64
WIDTH = 1024
CUT = 128
PLACES = 256
BF = jnp.bfloat16
F32 = jnp.float32
NT = (((1,), (1,)), ((), ()))
TN = (((0,), (0,)), ((), ()))


def columns(cores):
    return [
        [(zh * 4 + y) * 32 + x * 8 + zl * 2 + c for zh in range(2) for zl in range(4) for y in range(4) for c in cs]
        for x in range(4)
        for cs in ([(0, 1)] if cores == 2 else [(0,), (1,)])
    ]


def exchange(x, cores):
    return lax.all_to_all(
        x, ("grp", "dev"), split_axis=0, concat_axis=0, tiled=True, axis_index_groups=columns(cores)
    )


def spread(x, cores):
    return exchange(jnp.broadcast_to(x[None], (32 * cores, *x.shape)), cores)


def after(x, *others):
    return lax.optimization_barrier((x, *others))[0]


def call(kernel, out, flops, *args, where=None, scratch=(), hbm=(), mib=12):
    vmem = pl.BlockSpec(memory_space=pltpu.VMEM)
    first = [] if where is None else [where]
    return pl.pallas_call(
        kernel,
        out_shape=out,
        in_specs=[pl.BlockSpec(memory_space=pltpu.SMEM)] * len(first)
        + [pl.BlockSpec(memory_space=pltpu.HBM) if i in hbm else vmem for i in range(len(args))],
        out_specs=jax.tree.map(lambda _: vmem, out),
        scratch_shapes=list(scratch),
        compiler_params=pltpu.CompilerParams(vmem_limit_bytes=mib * 2**20),
        cost_estimate=pl.CostEstimate(flops=flops, bytes_accessed=2**20, transcendentals=0),
    )(*first, *args)


def shape(dims, kind):
    return jax.ShapeDtypeStruct(dims, kind)


def dot(a, b, dims=(((1,), (0,)), ((), ()))):
    return lax.dot_general(a, b, dims, preferred_element_type=F32)


def exact(a, b):
    return jnp.dot(a, b, preferred_element_type=F32, precision=lax.Precision.HIGHEST)


def terms(x):
    high = x.astype(BF)
    rest = x - high.astype(F32)
    mid = rest.astype(BF)
    return high, mid, (rest - mid.astype(F32)).astype(BF)


def head_mask(rows):
    row = lax.broadcasted_iota(jnp.int32, (rows, 4 * HEAD), 0)
    col = lax.broadcasted_iota(jnp.int32, (rows, 4 * HEAD), 1)
    return lax.rem(row, 4) == lax.div(col, HEAD)


def pick_kernel(where, info_ref, bank_ref, keep_ref, give_ref, select_ref):
    n = bank_ref.shape[0]
    number = lax.broadcasted_iota(jnp.int32, (PLACES, n), 1).astype(F32)
    own, slot, place = [info_ref[:, i : i + 1] for i in range(3)]
    a = jnp.where((place == number) & (own == where[6].astype(F32)), 1.0, 0.0).astype(BF)
    b = jnp.where(slot == number, 1.0, 0.0).astype(BF)
    select_ref[...] = dot(a, b, TN)
    for ref, c in ((keep_ref, where[3]), (give_ref, 1 - where[3])):
        half = pl.ds(pl.multiple_of(c * (PLACES // 2), PLACES // 2), PLACES // 2)
        ref[...] = dot(select_ref[half, :].astype(BF), bank_ref[...]).astype(BF)


def row_blocks(where):
    zh, y = where[0], where[1]
    for k in range(4):
        yk = lax.rem(y + 4 - k, 4)
        for h in range(2):
            at = ((zh if h == 0 else 1 - zh) * 4 + yk) * CUT
            yield k, slice(h * CUT, (h + 1) * CUT), pl.ds(pl.multiple_of(at, CUT), CUT)


def encode_kernel(
    where, h0, h1, h2, h3, n0, n1, n2, n3, f0, f1, f2, f3, out_ref, out2_ref, part_ref, w_ref
):
    near, far = (n0, n1, n2, n3), (f0, f1, f2, f3)
    for k, rows, features in row_blocks(where):
        for i in range(3):
            cols = slice(i * CUT, (i + 1) * CUT)
            w_ref[features, 2 * i * CUT : (2 * i + 1) * CUT] = near[k][rows, cols]
            w_ref[features, (2 * i + 1) * CUT : (2 * i + 2) * CUT] = far[k][rows, cols]
    four = 4 * HEAD
    mask = head_mask(4)
    contexts = []
    for ref in (h0, h1, h2, h3):
        x = ref[...]
        keyval = dot(x, w_ref[:, four:]).astype(BF)
        query = (0.125 * dot(x[0:16], w_ref[:, :four])[0:1]).astype(BF).astype(F32)
        query = jnp.where(mask, jnp.broadcast_to(query, (4, four)), 0.0).astype(BF)
        scores = dot(query, keyval[:, :four], NT)
        e = jnp.exp(scores - jnp.max(scores, axis=1, keepdims=True))
        probs = (e / jnp.sum(e, axis=1, keepdims=True)).astype(BF)
        context = jnp.where(mask, dot(probs, keyval[:, four:]), 0.0)
        contexts.append(jnp.sum(context, axis=0, keepdims=True))
    context = jnp.concatenate(contexts, axis=0).astype(BF)
    part = dot(context[:, :CUT], out_ref[...]) + dot(context[:, CUT:], out2_ref[...])
    for k in range(4):
        row = part[k : k + 1]
        if k == 0:
            row = row + h0[0:1, :].astype(F32)
        part_ref[pl.ds(lax.rem(where[2] + 4 - k, 4), 1), :] = row


def pack_kernel(part_ref, old_ref, both_ref):
    both_ref[...] = jnp.concatenate([part_ref[...], jnp.sum(old_ref[...].astype(F32), axis=0)], axis=0)


def norm_kernel(t0, t1, t2, t3, gain_ref, bias_ref, rows_ref):
    total = (t0[...] + t1[...]) + (t2[...] + t3[...])
    joined = total[0:4]
    center = joined - jnp.mean(joined, axis=-1, keepdims=True)
    var = jnp.mean(center * center, axis=-1, keepdims=True)
    normed = center / jnp.sqrt(var + 1e-05) * gain_ref[...] + bias_ref[...]
    fresh = normed / jnp.sqrt(jnp.mean(normed * normed, axis=-1, keepdims=True) + 1e-06)
    rows_ref[...] = jnp.concatenate([fresh, total[4:8]], axis=0).astype(BF)


def product(a, b):
    a1, a2, _ = terms(a)
    b1, b2, _ = terms(b)
    return dot(a2, b1) + dot(a1, b2) + dot(a1, b1)


def update_kernel(here_ref, there_ref, bank_ref, out_ref):
    half = here_ref.shape[0] // 2
    row = lax.broadcasted_iota(jnp.int32, (half, 2 * half), 0)
    col = lax.broadcasted_iota(jnp.int32, (half, 2 * half), 1)
    at = lax.div(row, 4) * 8 + lax.rem(row, 4)

    def take(first):
        pick = jnp.where(col == at + first, 1.0, 0.0).astype(BF)
        return jnp.concatenate([dot(pick, ref[...]).astype(BF) for ref in (here_ref, there_ref)], axis=0)

    old, fresh = take(4), take(0)
    n = 2 * half
    rows = lax.broadcasted_iota(jnp.int32, (n, n), 0)
    cols = lax.broadcasted_iota(jnp.int32, (n, n), 1)
    eye = jnp.where(rows == cols, 1.0, 0.0).astype(F32)
    ridge = 0.25 * n
    a = dot(old, old, NT) + ridge * eye
    norm = jnp.max(jnp.sum(jnp.abs(a), axis=1, keepdims=True))
    c = 2.0 / (ridge + norm)
    r = eye - c * a
    x = c * (eye + r)

    def size(r):
        return jnp.max(jnp.sum(jnp.abs(r), axis=1, keepdims=True))

    def step(times, state):
        t, _, x, r = state
        both = times(jnp.concatenate([x, r], axis=0), r)
        r = both[n:]
        return 2.0 * t, size(r), x + both[:n], r

    def more(state):
        return (state[0] < 7.0) & (state[1] > 1e-3)

    r = lax.cond(norm < 512.0 * ridge, product, exact, r, r)
    state = (2.0 * c * ridge, size(r), x, r)
    state = lax.while_loop(lambda s: more(s) & (norm < 512.0 * ridge), lambda s: step(product, s), state)
    x = lax.while_loop(more, lambda s: step(exact, s), state)[2]

    def refine(state):
        i, _, x = state
        e = eye - exact(a, x)
        return i + 1, jnp.sum(e * e), x + product(x, e)

    _, _, x = lax.while_loop(
        lambda s: (s[0] == 0) | ((s[1] > 1e-6) & (s[0] < 4)), refine, (jnp.int32(0), jnp.float32(1.0), x)
    )
    high, mid, low = terms(x)
    z1, z2, z3 = terms(dot(low, fresh) + dot(mid, fresh) + dot(high, fresh))
    adapter = (dot(old, z3, TN) + dot(old, z2, TN) + dot(old, z1, TN)).astype(BF)
    out_ref[...] = dot(bank_ref[...], adapter).astype(BF)


def shift(x, move):
    perm = []
    for i in range(256):
        zh, y, xx, zl, c = i // 128, i // 32 % 4, i // 8 % 4, i // 2 % 4, i % 2
        zh, y, xx, zl, c = move(zh, y, xx, zl, c)
        perm.append((i, (((zh % 2) * 4 + y % 4) * 4 + xx % 4) * 8 + (zl % 4) * 2 + c % 2))
    return lax.ppermute(x, ("grp", "dev"), perm)


def along_y(x, k):
    return shift(x, lambda zh, y, xx, zl, c: (zh, y + k, xx, zl, c)) if k % 4 else x


def along_x(x, k):
    return shift(x, lambda zh, y, xx, zl, c: (zh, y, xx + k, zl, c)) if k % 4 else x


def other_core(x):
    return shift(x, lambda zh, y, xx, zl, c: (zh, y, xx, zl, c + 1))


def mirror(x):
    return shift(x, lambda zh, y, xx, zl, c: (zh + 1, y, xx, 3 - zl, c))


def local(hidden_in, w_query, w_keyval, w_out, ln_gain, ln_bias, bank, owner, slot):
    hidden = hidden_in[0]
    grp, dev = lax.axis_index("grp"), lax.axis_index("dev")
    zh, y, x, zl, c = grp // 4, grp % 4, dev // 8, dev // 2 % 4, dev % 2
    where = jnp.stack([zh, y, x, c, owner[0], slot[0], grp * 32 + dev])

    h1, h3 = along_x(hidden, 1), along_x(hidden, 3)
    h2 = along_x(h1, 1)

    at = (4 * c + x) * CUT
    own = [(w_query, at), (w_keyval, at), (w_keyval, at + WIDTH)]
    own = jnp.concatenate([lax.dynamic_slice_in_dim(w, at, CUT, 1) for w, at in own], axis=1)
    out1 = shift(w_out, lambda zh, y, xx, zl, c: (c, xx, y, zl if c == zh else 3 - zl, zh))
    got = mirror(own)
    own = after(jnp.concatenate([own, got], axis=0), h1, h3, out1)
    out2 = other_core(out1)
    near = [along_y(own, k) for k in range(4)]
    near[0] = after(near[0], *near[1:], h2)
    far = [other_core(w) for w in near]

    place = (((c * 2 + zh) * 4 + zl) * 4 + y) * 4 + x
    lane = lax.broadcasted_iota(jnp.int32, (PLACES, 1, 128), 2)
    info = jnp.where(lane == 0, where[4], jnp.where(lane == 1, where[5], place)).astype(F32)
    info = lax.all_to_all(after(info, got), ("grp", "dev"), split_axis=0, concat_axis=0, tiled=True).reshape(PLACES, 128)
    half = shape((PLACES // 2, WIDTH), BF)
    keep, give = call(
        pick_kernel, [half, half], 2**27, info, bank, where=where, scratch=[pltpu.VMEM((PLACES, PLACES), F32)]
    )
    rows = keep + other_core(after(give, *near[1:]))
    rows = exchange(after(rows, *near[1:], h2).reshape(32, 4, WIDTH), 1)

    part = call(
        encode_kernel,
        shape((4, WIDTH), F32),
        2**30,
        hidden,
        h1,
        h2,
        h3,
        *near,
        *far,
        out1,
        out2,
        where=where,
        scratch=[pltpu.VMEM((WIDTH, 6 * CUT), BF)],
    )
    both = call(pack_kernel, shape((8, WIDTH), F32), 2**18, part, rows)
    both = [along_x(both, k) for k in range(4)]
    mine = call(
        norm_kernel, shape((8, WIDTH), BF), 2**14, *both, ln_gain.reshape(1, -1), ln_bias.reshape(1, -1)
    )
    here = spread(mine, 1)
    there = other_core(here)
    return call(
        update_kernel,
        shape(bank.shape, BF),
        2**31,
        here.reshape(256, WIDTH),
        there.reshape(256, WIDTH),
        bank,
        mib=24,
    )


def solution(mesh):
    in_specs = (
        P(("grp", "dev"), None, None),
        P("grp", None),
        P("grp", None),
        P("grp", None),
        P(),
        P(),
        P(("grp", "dev"), None),
        P(("grp", "dev")),
        P(("grp", "dev")),
    )
    out_specs = P(("grp", "dev"), None)
    return jax.shard_map(local, mesh=mesh, in_specs=in_specs, out_specs=out_specs, check_vma=False)
```

```python
import jax
import jax.numpy as jnp
from jax import lax
from jax.experimental import pallas as pl
from jax.experimental.pallas import tpu as pltpu
from jax.sharding import PartitionSpec as P

HEAD = 64
WIDTH = 1024
CUT = 128
PLACES = 256
BF = jnp.bfloat16
F32 = jnp.float32
NT = (((1,), (1,)), ((), ()))
TN = (((0,), (0,)), ((), ()))


def columns(cores):
    return [
        [(zh * 4 + y) * 32 + x * 8 + zl * 2 + c for zh in range(2) for zl in range(4) for y in range(4) for c in cs]
        for x in range(4)
        for cs in ([(0, 1)] if cores == 2 else [(0,), (1,)])
    ]


def exchange(x, cores):
    return lax.all_to_all(
        x, ("grp", "dev"), split_axis=0, concat_axis=0, tiled=True, axis_index_groups=columns(cores)
    )


def spread(x, cores):
    return exchange(jnp.broadcast_to(x[None], (32 * cores, *x.shape)), cores)


def after(x, *others):
    return lax.optimization_barrier((x, *others))[0]


def call(kernel, out, flops, *args, where=None, scratch=(), hbm=(), mib=12):
    vmem = pl.BlockSpec(memory_space=pltpu.VMEM)
    first = [] if where is None else [where]
    return pl.pallas_call(
        kernel,
        out_shape=out,
        in_specs=[pl.BlockSpec(memory_space=pltpu.SMEM)] * len(first)
        + [pl.BlockSpec(memory_space=pltpu.HBM) if i in hbm else vmem for i in range(len(args))],
        out_specs=jax.tree.map(lambda _: vmem, out),
        scratch_shapes=list(scratch),
        compiler_params=pltpu.CompilerParams(vmem_limit_bytes=mib * 2**20),
        cost_estimate=pl.CostEstimate(flops=flops, bytes_accessed=2**20, transcendentals=0),
    )(*first, *args)


def shape(dims, kind):
    return jax.ShapeDtypeStruct(dims, kind)


def dot(a, b, dims=(((1,), (0,)), ((), ()))):
    return lax.dot_general(a, b, dims, preferred_element_type=F32)


def exact(a, b):
    return jnp.dot(a, b, preferred_element_type=F32, precision=lax.Precision.HIGHEST)


def terms(x):
    high = x.astype(BF)
    rest = x - high.astype(F32)
    mid = rest.astype(BF)
    return high, mid, (rest - mid.astype(F32)).astype(BF)


def head_mask(rows):
    row = lax.broadcasted_iota(jnp.int32, (rows, 4 * HEAD), 0)
    col = lax.broadcasted_iota(jnp.int32, (rows, 4 * HEAD), 1)
    return lax.rem(row, 4) == lax.div(col, HEAD)


def pick_kernel(where, info_ref, bank_ref, keep_ref, give_ref, select_ref):
    n = bank_ref.shape[0]
    number = lax.broadcasted_iota(jnp.int32, (PLACES, n), 1).astype(F32)
    own, slot, place = [info_ref[:, i : i + 1] for i in range(3)]
    a = jnp.where((place == number) & (own == where[6].astype(F32)), 1.0, 0.0).astype(BF)
    b = jnp.where(slot == number, 1.0, 0.0).astype(BF)
    select_ref[...] = dot(a, b, TN)
    for ref, c in ((keep_ref, where[3]), (give_ref, 1 - where[3])):
        half = pl.ds(pl.multiple_of(c * (PLACES // 2), PLACES // 2), PLACES // 2)
        ref[...] = dot(select_ref[half, :].astype(BF), bank_ref[...]).astype(BF)


def row_blocks(where):
    zh, y = where[0], where[1]
    for k in range(4):
        yk = lax.rem(y + 4 - k, 4)
        for h in range(2):
            at = ((zh if h == 0 else 1 - zh) * 4 + yk) * CUT
            yield k, slice(h * CUT, (h + 1) * CUT), pl.ds(pl.multiple_of(at, CUT), CUT)


def encode_kernel(
    where, h0, h1, h2, h3, n0, n1, n2, n3, f0, f1, f2, f3, out_ref, out2_ref, part_ref, w_ref
):
    near, far = (n0, n1, n2, n3), (f0, f1, f2, f3)
    for k, rows, features in row_blocks(where):
        for i in range(3):
            cols = slice(i * CUT, (i + 1) * CUT)
            w_ref[features, 2 * i * CUT : (2 * i + 1) * CUT] = near[k][rows, cols]
            w_ref[features, (2 * i + 1) * CUT : (2 * i + 2) * CUT] = far[k][rows, cols]
    four = 4 * HEAD
    mask = head_mask(4)
    contexts = []
    for ref in (h0, h1, h2, h3):
        x = ref[...]
        keyval = dot(x, w_ref[:, four:]).astype(BF)
        query = (0.125 * dot(x[0:16], w_ref[:, :four])[0:1]).astype(BF).astype(F32)
        query = jnp.where(mask, jnp.broadcast_to(query, (4, four)), 0.0).astype(BF)
        scores = dot(query, keyval[:, :four], NT)
        e = jnp.exp(scores - jnp.max(scores, axis=1, keepdims=True))
        probs = (e / jnp.sum(e, axis=1, keepdims=True)).astype(BF)
        context = jnp.where(mask, dot(probs, keyval[:, four:]), 0.0)
        contexts.append(jnp.sum(context, axis=0, keepdims=True))
    context = jnp.concatenate(contexts, axis=0).astype(BF)
    part = dot(context[:, :CUT], out_ref[...]) + dot(context[:, CUT:], out2_ref[...])
    for k in range(4):
        row = part[k : k + 1]
        if k == 0:
            row = row + h0[0:1, :].astype(F32)
        part_ref[pl.ds(lax.rem(where[2] + 4 - k, 4), 1), :] = row


def pack_kernel(part_ref, old_ref, both_ref):
    both_ref[...] = jnp.concatenate([part_ref[...], jnp.sum(old_ref[...].astype(F32), axis=0)], axis=0)


def norm_kernel(t0, t1, t2, t3, gain_ref, bias_ref, rows_ref):
    total = (t0[...] + t1[...]) + (t2[...] + t3[...])
    joined = total[0:4]
    center = joined - jnp.mean(joined, axis=-1, keepdims=True)
    var = jnp.mean(center * center, axis=-1, keepdims=True)
    normed = center / jnp.sqrt(var + 1e-05) * gain_ref[...] + bias_ref[...]
    fresh = normed / jnp.sqrt(jnp.mean(normed * normed, axis=-1, keepdims=True) + 1e-06)
    rows_ref[...] = jnp.concatenate([fresh, total[4:8]], axis=0).astype(BF)


def product(a, b):
    a1, a2, _ = terms(a)
    b1, b2, _ = terms(b)
    return dot(a2, b1) + dot(a1, b2) + dot(a1, b1)


def update_kernel(here_ref, there_ref, bank_ref, out_ref):
    half = here_ref.shape[0] // 2
    row = lax.broadcasted_iota(jnp.int32, (half, 2 * half), 0)
    col = lax.broadcasted_iota(jnp.int32, (half, 2 * half), 1)
    at = lax.div(row, 4) * 8 + lax.rem(row, 4)

    def take(first):
        pick = jnp.where(col == at + first, 1.0, 0.0).astype(BF)
        return jnp.concatenate([dot(pick, ref[...]).astype(BF) for ref in (here_ref, there_ref)], axis=0)

    old, fresh = take(4), take(0)
    n = 2 * half
    rows = lax.broadcasted_iota(jnp.int32, (n, n), 0)
    cols = lax.broadcasted_iota(jnp.int32, (n, n), 1)
    eye = jnp.where(rows == cols, 1.0, 0.0).astype(F32)
    ridge = 0.25 * n
    a = dot(old, old, NT) + ridge * eye
    norm = jnp.max(jnp.sum(jnp.abs(a), axis=1, keepdims=True))
    c = 2.0 / (ridge + norm)
    r = eye - c * a
    x = c * (eye + r)

    def size(r):
        return jnp.max(jnp.sum(jnp.abs(r), axis=1, keepdims=True))

    def step(times, state):
        t, _, x, r = state
        both = times(jnp.concatenate([x, r], axis=0), r)
        r = both[n:]
        return 2.0 * t, size(r), x + both[:n], r

    def more(state):
        return (state[0] < 9.0) & (state[1] > 1e-4)

    r = exact(r, r)
    state = (2.0 * c * ridge, size(r), x, r)
    state = lax.while_loop(lambda s: more(s) & (norm < 512.0 * ridge), lambda s: step(product, s), state)
    x = lax.while_loop(more, lambda s: step(exact, s), state)[2]

    def refine(state):
        i, _, x = state
        e = eye - exact(a, x)
        return i + 1, jnp.sum(e * e), x + exact(x, e)

    _, _, x = lax.while_loop(
        lambda s: (s[0] == 0) | ((s[1] > 1e-7) & (s[0] < 4)), refine, (jnp.int32(0), jnp.float32(1.0), x)
    )
    high, mid, low = terms(x)
    z1, z2, z3 = terms(dot(low, fresh) + dot(mid, fresh) + dot(high, fresh))
    adapter = (dot(old, z3, TN) + dot(old, z2, TN) + dot(old, z1, TN)).astype(BF)
    out_ref[...] = dot(bank_ref[...], adapter).astype(BF)


def shift(x, move):
    perm = []
    for i in range(256):
        zh, y, xx, zl, c = i // 128, i // 32 % 4, i // 8 % 4, i // 2 % 4, i % 2
        zh, y, xx, zl, c = move(zh, y, xx, zl, c)
        perm.append((i, (((zh % 2) * 4 + y % 4) * 4 + xx % 4) * 8 + (zl % 4) * 2 + c % 2))
    return lax.ppermute(x, ("grp", "dev"), perm)


def along_y(x, k):
    return shift(x, lambda zh, y, xx, zl, c: (zh, y + k, xx, zl, c)) if k % 4 else x


def along_x(x, k):
    return shift(x, lambda zh, y, xx, zl, c: (zh, y, xx + k, zl, c)) if k % 4 else x


def other_core(x):
    return shift(x, lambda zh, y, xx, zl, c: (zh, y, xx, zl, c + 1))


def mirror(x):
    return shift(x, lambda zh, y, xx, zl, c: (zh + 1, y, xx, 3 - zl, c))


def local(hidden_in, w_query, w_keyval, w_out, ln_gain, ln_bias, bank, owner, slot):
    hidden = hidden_in[0]
    grp, dev = lax.axis_index("grp"), lax.axis_index("dev")
    zh, y, x, zl, c = grp // 4, grp % 4, dev // 8, dev // 2 % 4, dev % 2
    where = jnp.stack([zh, y, x, c, owner[0], slot[0], grp * 32 + dev])

    h1, h3 = along_x(hidden, 1), along_x(hidden, 3)
    h2 = along_x(h1, 1)

    at = (4 * c + x) * CUT
    own = [(w_query, at), (w_keyval, at), (w_keyval, at + WIDTH)]
    own = jnp.concatenate([lax.dynamic_slice_in_dim(w, at, CUT, 1) for w, at in own], axis=1)
    out1 = shift(w_out, lambda zh, y, xx, zl, c: (c, xx, y, zl if c == zh else 3 - zl, zh))
    got = mirror(own)
    own = after(jnp.concatenate([own, got], axis=0), h1, h3, out1)
    out2 = other_core(out1)
    near = [along_y(own, k) for k in range(4)]
    near[0] = after(near[0], *near[1:], h2)
    far = [other_core(w) for w in near]

    place = (((c * 2 + zh) * 4 + zl) * 4 + y) * 4 + x
    lane = lax.broadcasted_iota(jnp.int32, (PLACES, 1, 128), 2)
    info = jnp.where(lane == 0, where[4], jnp.where(lane == 1, where[5], place)).astype(F32)
    info = lax.all_to_all(after(info, got), ("grp", "dev"), split_axis=0, concat_axis=0, tiled=True).reshape(PLACES, 128)
    half = shape((PLACES // 2, WIDTH), BF)
    keep, give = call(
        pick_kernel, [half, half], 2**27, info, bank, where=where, scratch=[pltpu.VMEM((PLACES, PLACES), F32)]
    )
    rows = keep + other_core(after(give, *near[1:]))
    rows = exchange(after(rows, *near[1:], h2).reshape(32, 4, WIDTH), 1)

    here = jnp.stack([after(zh, h2), y, x, c])
    part = call(
        encode_kernel,
        shape((4, WIDTH), F32),
        2**30,
        hidden,
        h1,
        h2,
        h3,
        *near,
        *far,
        out1,
        out2,
        where=here,
        scratch=[pltpu.VMEM((WIDTH, 6 * CUT), BF)],
    )
    both = call(pack_kernel, shape((8, WIDTH), F32), 2**18, part, rows)
    both = [along_x(both, k) for k in range(4)]
    mine = call(
        norm_kernel, shape((8, WIDTH), BF), 2**14, *both, ln_gain.reshape(1, -1), ln_bias.reshape(1, -1)
    )
    here = spread(mine, 1)
    there = other_core(here)
    return call(
        update_kernel,
        shape(bank.shape, BF),
        2**31,
        here.reshape(256, WIDTH),
        there.reshape(256, WIDTH),
        bank,
        mib=24,
    )


def solution(mesh):
    in_specs = (
        P(("grp", "dev"), None, None),
        P("grp", None),
        P("grp", None),
        P("grp", None),
        P(),
        P(),
        P(("grp", "dev"), None),
        P(("grp", "dev")),
        P(("grp", "dev")),
    )
    out_specs = P(("grp", "dev"), None)
    return jax.shard_map(local, mesh=mesh, in_specs=in_specs, out_specs=out_specs, check_vma=False)
```

```python
import jax
import jax.numpy as jnp
from jax import lax
from jax.experimental import pallas as pl
from jax.experimental.pallas import tpu as pltpu
from jax.sharding import PartitionSpec as P

HEAD = 64
WIDTH = 1024
CUT = 128
PLACES = 256
BF = jnp.bfloat16
F32 = jnp.float32
NT = (((1,), (1,)), ((), ()))
TN = (((0,), (0,)), ((), ()))


def columns(cores):
    return [
        [(zh * 4 + y) * 32 + x * 8 + zl * 2 + c for zh in range(2) for zl in range(4) for y in range(4) for c in cs]
        for x in range(4)
        for cs in ([(0, 1)] if cores == 2 else [(0,), (1,)])
    ]


def exchange(x, cores):
    return lax.all_to_all(
        x, ("grp", "dev"), split_axis=0, concat_axis=0, tiled=True, axis_index_groups=columns(cores)
    )


def spread(x, cores):
    return exchange(jnp.broadcast_to(x[None], (32 * cores, *x.shape)), cores)


def after(x, *others):
    return lax.optimization_barrier((x, *others))[0]


def call(kernel, out, flops, *args, where=None, scratch=(), hbm=(), mib=12):
    vmem = pl.BlockSpec(memory_space=pltpu.VMEM)
    first = [] if where is None else [where]
    return pl.pallas_call(
        kernel,
        out_shape=out,
        in_specs=[pl.BlockSpec(memory_space=pltpu.SMEM)] * len(first)
        + [pl.BlockSpec(memory_space=pltpu.HBM) if i in hbm else vmem for i in range(len(args))],
        out_specs=jax.tree.map(lambda _: vmem, out),
        scratch_shapes=list(scratch),
        compiler_params=pltpu.CompilerParams(vmem_limit_bytes=mib * 2**20),
        cost_estimate=pl.CostEstimate(flops=flops, bytes_accessed=2**20, transcendentals=0),
    )(*first, *args)


def shape(dims, kind):
    return jax.ShapeDtypeStruct(dims, kind)


def dot(a, b, dims=(((1,), (0,)), ((), ()))):
    return lax.dot_general(a, b, dims, preferred_element_type=F32)


def exact(a, b):
    return jnp.dot(a, b, preferred_element_type=F32, precision=lax.Precision.HIGHEST)


def terms(x):
    high = x.astype(BF)
    rest = x - high.astype(F32)
    mid = rest.astype(BF)
    return high, mid, (rest - mid.astype(F32)).astype(BF)


def head_mask(rows):
    row = lax.broadcasted_iota(jnp.int32, (rows, 4 * HEAD), 0)
    col = lax.broadcasted_iota(jnp.int32, (rows, 4 * HEAD), 1)
    return lax.rem(row, 4) == lax.div(col, HEAD)


def cut_kernel(where, query_ref, keyval_ref, own_ref):
    block = 4 * where[3] + where[2]
    at = pl.ds(pl.multiple_of(block * CUT, CUT), CUT)
    own_ref[:, :CUT] = query_ref[:, at]
    own_ref[:, CUT : 2 * CUT] = keyval_ref[:, at]
    own_ref[:, 2 * CUT :] = keyval_ref[:, pl.ds(pl.multiple_of(block * CUT + WIDTH, CUT), CUT)]


def pick_kernel(where, info_ref, bank_ref, keep_ref, give_ref, select_ref):
    n = bank_ref.shape[0]
    number = lax.broadcasted_iota(jnp.int32, (PLACES, n), 1).astype(F32)
    own, slot, place = [info_ref[:, i : i + 1] for i in range(3)]
    a = jnp.where((place == number) & (own == where[6].astype(F32)), 1.0, 0.0).astype(BF)
    b = jnp.where(slot == number, 1.0, 0.0).astype(BF)
    select_ref[...] = dot(a, b, TN)
    for ref, c in ((keep_ref, where[3]), (give_ref, 1 - where[3])):
        half = pl.ds(pl.multiple_of(c * (PLACES // 2), PLACES // 2), PLACES // 2)
        ref[...] = dot(select_ref[half, :].astype(BF), bank_ref[...]).astype(BF)


def row_blocks(where):
    zh, y = where[0], where[1]
    for k in range(4):
        yk = lax.rem(y + 4 - k, 4)
        for h in range(2):
            at = ((zh if h == 0 else 1 - zh) * 4 + yk) * CUT
            yield k, slice(h * CUT, (h + 1) * CUT), pl.ds(pl.multiple_of(at, CUT), CUT)


def encode_kernel(
    where, h0, h1, h2, h3, n0, n1, n2, n3, f0, f1, f2, f3, out_ref, out2_ref, part_ref, w_ref
):
    near, far = (n0, n1, n2, n3), (f0, f1, f2, f3)
    for k, rows, features in row_blocks(where):
        for i in range(3):
            cols = slice(i * CUT, (i + 1) * CUT)
            w_ref[features, 2 * i * CUT : (2 * i + 1) * CUT] = near[k][rows, cols]
            w_ref[features, (2 * i + 1) * CUT : (2 * i + 2) * CUT] = far[k][rows, cols]
    four = 4 * HEAD
    mask = head_mask(4)
    contexts = []
    for ref in (h0, h1, h2, h3):
        x = ref[...]
        keyval = dot(x, w_ref[:, four:]).astype(BF)
        query = (0.125 * dot(x[0:16], w_ref[:, :four])[0:1]).astype(BF).astype(F32)
        query = jnp.where(mask, jnp.broadcast_to(query, (4, four)), 0.0).astype(BF)
        scores = dot(query, keyval[:, :four], NT)
        e = jnp.exp(scores - jnp.max(scores, axis=1, keepdims=True))
        probs = (e / jnp.sum(e, axis=1, keepdims=True)).astype(BF)
        context = jnp.where(mask, dot(probs, keyval[:, four:]), 0.0)
        contexts.append(jnp.sum(context, axis=0, keepdims=True))
    context = jnp.concatenate(contexts, axis=0).astype(BF)
    part = dot(context[:, :CUT], out_ref[...]) + dot(context[:, CUT:], out2_ref[...])
    for k in range(4):
        row = part[k : k + 1]
        if k == 0:
            row = row + h0[0:1, :].astype(F32)
        part_ref[pl.ds(lax.rem(where[2] + 4 - k, 4), 1), :] = row


def pack_kernel(part_ref, old_ref, both_ref):
    both_ref[...] = jnp.concatenate([part_ref[...], jnp.sum(old_ref[...].astype(F32), axis=0)], axis=0)


def norm_kernel(t0, t1, t2, t3, gain_ref, bias_ref, rows_ref):
    total = (t0[...] + t1[...]) + (t2[...] + t3[...])
    joined = total[0:4]
    center = joined - jnp.mean(joined, axis=-1, keepdims=True)
    var = jnp.mean(center * center, axis=-1, keepdims=True)
    normed = center / jnp.sqrt(var + 1e-05) * gain_ref[...] + bias_ref[...]
    fresh = normed / jnp.sqrt(jnp.mean(normed * normed, axis=-1, keepdims=True) + 1e-06)
    rows_ref[...] = jnp.concatenate([fresh, total[4:8]], axis=0).astype(BF)


def product(a, b):
    a1, a2, _ = terms(a)
    b1, b2, _ = terms(b)
    return dot(a2, b1) + dot(a1, b2) + dot(a1, b1)


def update_kernel(here_ref, there_ref, bank_ref, out_ref):
    half = here_ref.shape[0] // 2
    row = lax.broadcasted_iota(jnp.int32, (half, 2 * half), 0)
    col = lax.broadcasted_iota(jnp.int32, (half, 2 * half), 1)
    at = lax.div(row, 4) * 8 + lax.rem(row, 4)

    def take(first):
        pick = jnp.where(col == at + first, 1.0, 0.0).astype(BF)
        return jnp.concatenate([dot(pick, ref[...]).astype(BF) for ref in (here_ref, there_ref)], axis=0)

    old, fresh = take(4), take(0)
    n = 2 * half
    rows = lax.broadcasted_iota(jnp.int32, (n, n), 0)
    cols = lax.broadcasted_iota(jnp.int32, (n, n), 1)
    eye = jnp.where(rows == cols, 1.0, 0.0).astype(F32)
    ridge = 0.25 * n
    a = dot(old, old, NT) + ridge * eye
    norm = jnp.max(jnp.sum(jnp.abs(a), axis=1, keepdims=True))
    c = 2.0 / (ridge + norm)
    r = eye - c * a
    x = c * (eye + r)

    def size(r):
        return jnp.max(jnp.sum(jnp.abs(r), axis=1, keepdims=True))

    def step(times, state):
        t, _, x, r = state
        both = times(jnp.concatenate([x, r], axis=0), r)
        r = both[n:]
        return 2.0 * t, size(r), x + both[:n], r

    def more(state):
        return (state[0] < 9.0) & (state[1] > 1e-4)

    r = lax.cond(norm < 512.0 * ridge, product, exact, r, r)
    state = (2.0 * c * ridge, size(r), x, r)
    state = lax.while_loop(lambda s: more(s) & (norm < 512.0 * ridge), lambda s: step(product, s), state)
    x = lax.while_loop(more, lambda s: step(exact, s), state)[2]

    def refine(state):
        i, _, x = state
        e = eye - exact(a, x)
        return i + 1, jnp.sum(e * e), x + product(x, e)

    _, _, x = lax.while_loop(
        lambda s: (s[0] == 0) | ((s[1] > 1e-7) & (s[0] < 4)), refine, (jnp.int32(0), jnp.float32(1.0), x)
    )
    high, mid, low = terms(x)
    z1, z2, z3 = terms(dot(low, fresh) + dot(mid, fresh) + dot(high, fresh))
    adapter = (dot(old, z3, TN) + dot(old, z2, TN) + dot(old, z1, TN)).astype(BF)
    out_ref[...] = dot(bank_ref[...], adapter).astype(BF)


def shift(x, move):
    perm = []
    for i in range(256):
        zh, y, xx, zl, c = i // 128, i // 32 % 4, i // 8 % 4, i // 2 % 4, i % 2
        zh, y, xx, zl, c = move(zh, y, xx, zl, c)
        perm.append((i, (((zh % 2) * 4 + y % 4) * 4 + xx % 4) * 8 + (zl % 4) * 2 + c % 2))
    return lax.ppermute(x, ("grp", "dev"), perm)


def along_y(x, k):
    return shift(x, lambda zh, y, xx, zl, c: (zh, y + k, xx, zl, c)) if k % 4 else x


def along_x(x, k):
    return shift(x, lambda zh, y, xx, zl, c: (zh, y, xx + k, zl, c)) if k % 4 else x


def other_core(x):
    return shift(x, lambda zh, y, xx, zl, c: (zh, y, xx, zl, c + 1))


def mirror(x):
    return shift(x, lambda zh, y, xx, zl, c: (zh + 1, y, xx, 3 - zl, c))


def local(hidden_in, w_query, w_keyval, w_out, ln_gain, ln_bias, bank, owner, slot):
    hidden = hidden_in[0]
    grp, dev = lax.axis_index("grp"), lax.axis_index("dev")
    zh, y, x, zl, c = grp // 4, grp % 4, dev // 8, dev // 2 % 4, dev % 2
    where = jnp.stack([zh, y, x, c, owner[0], slot[0], grp * 32 + dev])

    h1, h3 = along_x(hidden, 1), along_x(hidden, 3)
    h2 = along_x(h1, 1)

    own = call(cut_kernel, shape((CUT, 3 * CUT), BF), 2**10, w_query, w_keyval, where=where)
    out1 = shift(w_out, lambda zh, y, xx, zl, c: (c, xx, y, zl if c == zh else 3 - zl, zh))
    got = mirror(own)
    own = after(jnp.concatenate([own, got], axis=0), h1, h3, out1)
    out2 = other_core(out1)
    near = [along_y(own, k) for k in range(4)]
    near[0] = after(near[0], *near[1:], h2)
    far = [other_core(w) for w in near]

    place = (((c * 2 + zh) * 4 + zl) * 4 + y) * 4 + x
    lane = lax.broadcasted_iota(jnp.int32, (PLACES, 1, 128), 2)
    info = jnp.where(lane == 0, where[4], jnp.where(lane == 1, where[5], place)).astype(F32)
    info = lax.all_to_all(after(info, got), ("grp", "dev"), split_axis=0, concat_axis=0, tiled=True).reshape(PLACES, 128)
    half = shape((PLACES // 2, WIDTH), BF)
    keep, give = call(
        pick_kernel, [half, half], 2**27, info, bank, where=where, scratch=[pltpu.VMEM((PLACES, PLACES), F32)]
    )
    rows = keep + other_core(after(give, *near[1:]))
    rows = exchange(after(rows, *near[1:], h2).reshape(32, 4, WIDTH), 1)

    part = call(
        encode_kernel,
        shape((4, WIDTH), F32),
        2**30,
        hidden,
        h1,
        h2,
        h3,
        *near,
        *far,
        out1,
        out2,
        where=where,
        scratch=[pltpu.VMEM((WIDTH, 6 * CUT), BF)],
    )
    both = call(pack_kernel, shape((8, WIDTH), F32), 2**18, part, rows)
    both = [along_x(both, k) for k in range(4)]
    mine = call(
        norm_kernel, shape((8, WIDTH), BF), 2**14, *both, ln_gain.reshape(1, -1), ln_bias.reshape(1, -1)
    )
    here = spread(mine, 1)
    there = other_core(here)
    return call(
        update_kernel,
        shape(bank.shape, BF),
        2**31,
        here.reshape(256, WIDTH),
        there.reshape(256, WIDTH),
        bank,
        mib=24,
    )


def solution(mesh):
    in_specs = (
        P(("grp", "dev"), None, None),
        P("grp", None),
        P("grp", None),
        P("grp", None),
        P(),
        P(),
        P(("grp", "dev"), None),
        P(("grp", "dev")),
        P(("grp", "dev")),
    )
    out_specs = P(("grp", "dev"), None)
    return jax.shard_map(local, mesh=mesh, in_specs=in_specs, out_specs=out_specs, check_vma=False)
```
